256 devices in a mesh: chan: 16 (over z, core), ctx: 16 (over x, y).
Axes of the slice: x: 4, y: 4, z: 8, core: 2. Of those that a mesh axis runs over, the one named last changes fastest.
Arguments:
- saved_input: float32 [2, 256, 131072], P(None, 'chan', 'ctx'), may hold values from -6 to 6
- out_grad: float32 [2, 256, 131072], P(None, 'chan', 'ctx'), may hold values from -6 to 6
- filters: float32 [2, 131072], P(None, 'ctx'), may hold values from -0.015625 to 0.015625
Outputs:
- input_grad: bfloat16 [2, 256, 131072], P(None, 'chan', 'ctx')
- filter_grad: float32 [2, 131072], P(None, 'ctx')
The draws below stay inside these ranges and needn't reach their ends.
All inputs are finite; a program needn't handle non-finite values.
Results may differ from the reference program's by a relative error of at most 0.001.
Values sent between devices are 32-bit elements; how exact they have to be, the bound alone decides.
No kernel may reach another device: no remote copies, remote signals or barrier semaphores. Data moves between devices by JAX's collectives and lax.ppermute only.
A program may use at most 128 MiB of HBM per device.

```python
import jax
import jax.numpy as jnp
from jax import lax

BATCH = 2
GROUPS = 2
CHANNELS = 256
LENGTH = 131072


def level_of(rng, dims, cuts, low, top_value):
    def one(position, parts):
        heights = jax.random.uniform(jax.random.fold_in(jax.random.fold_in(rng, 6), position), (parts,), jnp.float32, low / len(cuts), top_value / len(cuts))
        return jnp.repeat(jnp.exp(heights), dims[position] // parts).reshape((-1,) + (1,) * (len(dims) - position - 1))

    loudness = one(*cuts[0])
    for cut in cuts[1:]:
        loudness = loudness * one(*cut)
    return loudness


def scatter_about(stream_key, extent, scale, bound, pieces=(), held_as=jnp.bfloat16):
    factor_of = level_of(stream_key, extent, pieces, -0.22, 0.18) if pieces else 1.0
    array = jax.random.normal(stream_key, extent, jnp.float32) * scale * factor_of
    return jnp.minimum(jnp.maximum(array, -bound), bound).astype(held_as)


def setup_inputs(seed: int = 0) -> dict:
    arg_keys = jax.random.split(jax.random.key(seed), 4)
    return {
        "saved_input": scatter_about(arg_keys[0], (BATCH, CHANNELS, LENGTH), 1.0, 6.0, ((1, 16), (2, 16)), jnp.float32),
        "out_grad": scatter_about(arg_keys[1], (BATCH, CHANNELS, LENGTH), 1.0, 6.0, ((1, 16), (2, 16)), jnp.float32),
        "filters": scatter_about(arg_keys[2], (GROUPS, LENGTH), LENGTH ** -0.5, 0.015625, ((1, 16),), jnp.float32),
    }


def reference(saved_input, out_grad, filters):
    points = 2 * LENGTH
    per_filter = CHANNELS // GROUPS
    filter_spec = jnp.fft.rfft(filters.astype(jnp.float32), n=points, axis=-1)
    inputs = saved_input.astype(jnp.float32).reshape(BATCH, per_filter, GROUPS, LENGTH).transpose(1, 0, 2, 3)
    gradients = out_grad.astype(jnp.float32).reshape(BATCH, per_filter, GROUPS, LENGTH).transpose(1, 0, 2, 3)

    def one_block(running, block_pair):
        block_in, block_grad = block_pair
        in_spec = jnp.fft.rfft(block_in, n=points, axis=-1)
        grad_spec = jnp.fft.rfft(block_grad, n=points, axis=-1)
        input_part = jnp.fft.irfft(jnp.conj(filter_spec)[None] * grad_spec, n=points, axis=-1)[..., :LENGTH]
        filter_part = jnp.fft.irfft(jnp.sum(jnp.conj(in_spec) * grad_spec, axis=0), n=points, axis=-1)[..., :LENGTH]
        return running + filter_part, input_part.astype(jnp.bfloat16)

    filter_total, input_blocks = lax.scan(one_block, jnp.zeros((GROUPS, LENGTH), jnp.float32), (inputs, gradients))
    input_grad = input_blocks.transpose(1, 0, 2, 3).reshape(BATCH, CHANNELS, LENGTH)
    norm_factor = float(LENGTH * BATCH * per_filter) ** -0.5
    return input_grad, filter_total * norm_factor
```

```python
import functools
import math

import jax
import jax.numpy as jnp
import ml_dtypes
import numpy as np
from jax import lax
from jax.experimental import pallas as pl
from jax.experimental.pallas import tpu as pltpu
from jax.sharding import PartitionSpec as P

RADIX = 8
SIDE = 128
TOKENS = RADIX * SIDE * SIDE
LANES = 128
STEP = 16


def real_form(matrix):
    return np.block([[matrix.real, -matrix.imag], [matrix.imag, matrix.real]])


def two_halves(matrix):
    high = matrix.astype(ml_dtypes.bfloat16)
    low = (matrix - high.astype(np.float64)).astype(ml_dtypes.bfloat16)
    return np.stack([high, low])


@functools.cache
def tables():
    q = np.arange(RADIX)[:, None, None]
    first = np.arange(SIDE)[None, :, None]
    second = np.arange(SIDE)[None, None, :]
    turn = np.pi / 16 + np.pi * q / 4 + 2 * np.pi * first
    over_s = np.exp(1j * second * turn / SIDE)
    twiddle = np.exp(1j * second * turn / (SIDE * SIDE))
    over_l = np.exp(2j * np.pi * np.outer(np.arange(SIDE), np.arange(SIDE)) / SIDE)
    forward_s = np.stack([two_halves(real_form(m)) for m in over_s])
    inverse_s = np.stack([two_halves(real_form(m).T) for m in over_s])
    forward_l = two_halves(real_form(over_l).T)
    inverse_l = two_halves(real_form(over_l))
    turns = np.stack([twiddle.real, twiddle.imag], axis=1).astype(np.float32)
    return forward_s, inverse_s, forward_l, inverse_l, turns


def dft4(a, b, c, d, sign):
    t0 = (a[0] + c[0], a[1] + c[1])
    t1 = (a[0] - c[0], a[1] - c[1])
    t2 = (b[0] + d[0], b[1] + d[1])
    t3 = (b[0] - d[0], b[1] - d[1])
    if sign < 0:
        t3 = (-t3[0], -t3[1])
    return [
        (t0[0] + t2[0], t0[1] + t2[1]),
        (t1[0] - t3[1], t1[1] + t3[0]),
        (t0[0] - t2[0], t0[1] - t2[1]),
        (t1[0] + t3[1], t1[1] - t3[0]),
    ]


def dft8(u, sign):
    even = dft4(u[0], u[2], u[4], u[6], sign)
    odd = dft4(u[1], u[3], u[5], u[7], sign)
    half = math.sqrt(0.5)
    turned = [
        odd[0],
        (half * (odd[1][0] - sign * odd[1][1]), half * (odd[1][1] + sign * odd[1][0])),
        (-sign * odd[2][1], sign * odd[2][0]),
        (half * (-odd[3][0] - sign * odd[3][1]), half * (sign * odd[3][0] - odd[3][1])),
    ]
    plus = [(e[0] + o[0], e[1] + o[1]) for e, o in zip(even, turned)]
    minus = [(e[0] - o[0], e[1] - o[1]) for e, o in zip(even, turned)]
    return plus + minus


def split(values):
    high = values.astype(jnp.bfloat16)
    low = (values - high.astype(jnp.float32)).astype(jnp.bfloat16)
    return high, low


def dot(left, right):
    return jnp.dot(left, right, preferred_element_type=jnp.float32)


def dot_from_left(table_high, table_low, high, low):
    return dot(table_high, high) + dot(table_high, low) + dot(table_low, high)


def dot_from_right(high, low, table_high, table_low):
    return dot(high, table_high) + dot(low, table_high) + dot(high, table_low)


def radix_forward(rows_ref, first_row, count, high_ref, low_ref):
    per_block = rows_ref.shape[2] // STEP

    def body(step, carry):
        odd_half = step // per_block
        inner = pl.multiple_of((step % per_block) * STEP, STEP)
        target = pl.multiple_of(step * STEP, STEP)
        for row in range(count):
            u = []
            for r in range(RADIX):
                x = rows_ref[2 * r + odd_half, first_row + row, pl.ds(inner, STEP), :]
                angle = math.pi * r / 16
                u.append((math.cos(angle) * x, math.sin(angle) * x) if r else (x, jnp.zeros_like(x)))
            for q, value in enumerate(dft8(u, 1)):
                for part in range(2):
                    high, low = split(value[part])
                    lanes = pl.ds(row * LANES, LANES)
                    high_ref[q, part, pl.ds(target, STEP), lanes] = high
                    low_ref[q, part, pl.ds(target, STEP), lanes] = low
        return carry

    lax.fori_loop(0, SIDE // STEP, body, 0)


def radix_inverse(values_ref, count, store):
    per_block = SIDE // 2 // STEP

    def body(step, carry):
        odd_half = step // per_block
        inner = pl.multiple_of((step % per_block) * STEP, STEP)
        source = pl.multiple_of(step * STEP, STEP)
        for row in range(count):
            lanes = pl.ds(row * LANES, LANES)
            v = [
                tuple(values_ref[q, part, pl.ds(source, STEP), lanes] for part in range(2))
                for q in range(RADIX)
            ]
            for r, value in enumerate(dft8(v, -1)):
                angle = math.pi * r / 16
                real = math.cos(angle) * value[0] + math.sin(angle) * value[1] if r else value[0]
                store(2 * r + odd_half, row, pl.ds(inner, STEP), real)
        return carry

    lax.fori_loop(0, SIDE // STEP, body, 0)


def spectra_of(q, count, high_ref, low_ref, forward_s, forward_l, turns):
    high = high_ref[q].reshape(2 * SIDE, count * LANES)
    low = low_ref[q].reshape(2 * SIDE, count * LANES)
    z = dot_from_left(forward_s[q, 0], forward_s[q, 1], high, low)
    cosine, sine = turns[q, 0], turns[q, 1]
    rows = []
    for row in range(count):
        real = z[:SIDE, row * LANES : (row + 1) * LANES]
        imag = z[SIDE:, row * LANES : (row + 1) * LANES]
        rows.append(
            jnp.concatenate([real * cosine - imag * sine, real * sine + imag * cosine], axis=1)
        )
    high, low = split(jnp.concatenate(rows, axis=0))
    return dot_from_right(high, low, forward_l[0], forward_l[1])


def back_to_s(q, count, products, inverse_s, inverse_l, turns):
    high, low = split(products)
    u = dot_from_right(high, low, inverse_l[0], inverse_l[1])
    cosine, sine = turns[q, 0], turns[q, 1]
    rows = []
    for row in range(count):
        real = u[row * SIDE : (row + 1) * SIDE, :LANES]
        imag = u[row * SIDE : (row + 1) * SIDE, LANES:]
        rows.append(
            jnp.concatenate([real * cosine + imag * sine, imag * cosine - real * sine], axis=0)
        )
    high, low = split(jnp.concatenate(rows, axis=1))
    return dot_from_left(inverse_s[q, 0], inverse_s[q, 1], high, low)


def times_conjugate(a, b):
    ar, ai, br, bi = a[:, :LANES], a[:, LANES:], b[:, :LANES], b[:, LANES:]
    return ar * br + ai * bi, ai * br - ar * bi


def filter_kernel(
    rows, forward_s, inverse_s, forward_l, inverse_l, turns, terms, grads, high, low, back
):
    radix_forward(rows, 0, 4, high, low)

    def body(q, carry):
        spectra = spectra_of(q, 4, high, low, forward_s, forward_l, turns)
        grads[q] = spectra[2 * SIDE :]
        first = times_conjugate(spectra[2 * SIDE : 3 * SIDE], spectra[:SIDE])
        second = times_conjugate(spectra[3 * SIDE :], spectra[SIDE : 2 * SIDE])
        products = jnp.concatenate([first[0] + second[0], first[1] + second[1]], axis=1)
        out = back_to_s(q, 1, products, inverse_s, inverse_l, turns)
        back[q] = out.reshape(2, SIDE, LANES)
        return carry

    lax.fori_loop(0, RADIX, body, 0)

    def store(block, row, span, value):
        terms[block, span, :] = value

    radix_inverse(back, 1, store)


def input_kernel(
    rows, grads, forward_s, inverse_s, forward_l, inverse_l, turns, out, high, low, back
):
    radix_forward(rows, 4, 1, high, low)

    def body(q, carry):
        spectrum = spectra_of(q, 1, high, low, forward_s, forward_l, turns)
        products = jnp.concatenate(
            [
                jnp.concatenate(times_conjugate(grads[q, b * SIDE : (b + 1) * SIDE], spectrum), axis=1)
                for b in range(2)
            ],
            axis=0,
        )
        values = back_to_s(q, 2, products, inverse_s, inverse_l, turns)
        back[q] = values.reshape(2, SIDE, 2 * LANES)
        return carry

    lax.fori_loop(0, RADIX, body, 0)

    def store(block, row, span, value):
        out[block, row, span, :] = value

    radix_inverse(back, 2, store)


def in_vmem(count):
    return [pl.BlockSpec(memory_space=pltpu.VMEM)] * count


def scratch(rows_in, rows_back):
    return [
        pltpu.VMEM((RADIX, 2, SIDE, rows_in * LANES), jnp.bfloat16),
        pltpu.VMEM((RADIX, 2, SIDE, rows_in * LANES), jnp.bfloat16),
        pltpu.VMEM((RADIX, 2, SIDE, rows_back * LANES), jnp.float32),
    ]


def filter_terms(rows, consts):
    blocks = rows.shape[0]
    return pl.pallas_call(
        filter_kernel,
        out_shape=(
            jax.ShapeDtypeStruct((blocks, rows.shape[2], LANES), jnp.float32),
            jax.ShapeDtypeStruct((RADIX, 2 * SIDE, 2 * LANES), jnp.float32),
        ),
        in_specs=in_vmem(6),
        out_specs=tuple(in_vmem(2)),
        scratch_shapes=scratch(4, 1),
        compiler_params=pltpu.CompilerParams(vmem_limit_bytes=28 << 20),
        cost_estimate=pl.CostEstimate(
            flops=4_000_000_000, bytes_accessed=10_000_000, transcendentals=0
        ),
        name="filter_terms",
    )(rows, *consts)


def input_rows(rows, grads, consts):
    blocks = rows.shape[0]
    return pl.pallas_call(
        input_kernel,
        out_shape=jax.ShapeDtypeStruct((blocks, 2, rows.shape[2], LANES), jnp.float32),
        in_specs=in_vmem(7),
        out_specs=in_vmem(1)[0],
        scratch_shapes=scratch(1, 2),
        compiler_params=pltpu.CompilerParams(vmem_limit_bytes=28 << 20),
        cost_estimate=pl.CostEstimate(
            flops=2_500_000_000, bytes_accessed=10_000_000, transcendentals=0
        ),
        name="input_rows",
    )(rows, grads, *consts)


def local(saved_input, out_grad, filters):
    batch, channels, tokens = saved_input.shape
    groups = filters.shape[0]
    devices = lax.axis_size("ctx")
    chan = lax.axis_size("chan")
    chunks = tokens // LANES
    consts = tuple(jnp.asarray(t) for t in tables())
    shape = (batch, channels, chunks, LANES)
    by_channel = [jnp.swapaxes(v.reshape(shape), 0, 1) for v in (saved_input, out_grad)]
    own_filter = jnp.tile(filters.reshape(groups, 1, chunks, LANES), (channels // groups, 1, 1, 1))
    packed = jnp.concatenate([*by_channel, own_filter], axis=1)
    rows = lax.all_to_all(packed, "ctx", 0, 0, tiled=True)
    terms, grads = filter_terms(rows, consts)
    terms = lax.all_to_all(terms, "ctx", 0, 0, tiled=True)
    inputs = input_rows(rows, grads, consts)
    total = jnp.sum(terms.reshape(devices // groups, groups, chunks, LANES), axis=0)
    inputs, total = lax.optimization_barrier((inputs, total))
    inputs = lax.all_to_all(inputs, "ctx", 0, 0, tiled=True)
    hop = 1
    while hop < chan:
        total = total + lax.ppermute(total, "chan", [(i, i ^ hop) for i in range(chan)])
        hop *= 2
    per_filter = channels // groups
    norm = float(tokens * devices * batch * per_filter * chan) ** -0.5
    filter_grad = total.reshape(groups, tokens) * (norm / TOKENS)
    input_grad = jnp.swapaxes(inputs * (1.0 / TOKENS), 0, 1).reshape(batch, channels, tokens)
    return input_grad.astype(jnp.bfloat16), filter_grad


def solution(mesh):
    placed = (P(None, "chan", "ctx"), P(None, "chan", "ctx"), P(None, "ctx"))
    return jax.shard_map(
        local,
        mesh=mesh,
        in_specs=placed,
        out_specs=(P(None, "chan", "ctx"), P(None, "ctx")),
        check_vma=False,
    )
```

```python
import functools
import math

import jax
import jax.numpy as jnp
import ml_dtypes
import numpy as np
from jax import lax
from jax.experimental import pallas as pl
from jax.experimental.pallas import tpu as pltpu
from jax.sharding import PartitionSpec as P

RADIX = 8
SIDE = 128
TOKENS = RADIX * SIDE * SIDE
LANES = 128
STEP = 32


def two_halves(matrix):
    high = matrix.astype(ml_dtypes.bfloat16)
    low = (matrix - high.astype(np.float64)).astype(ml_dtypes.bfloat16)
    return high, low


@functools.cache
def tables():
    side = np.arange(SIDE)
    turn = np.pi / 2 + 2 * np.pi * side
    forward_s, inverse_s = [], []
    for r in range(RADIX):
        matrix = np.exp(1j * np.outer(turn, side + r / RADIX) / SIDE)
        high, low = two_halves(np.concatenate([matrix.real, matrix.imag], axis=0))
        forward_s.append(
            np.block([[high, high], [low, np.zeros_like(low)]]).astype(ml_dtypes.bfloat16)
        )
        high, low = two_halves(np.concatenate([matrix.real.T, matrix.imag.T], axis=1))
        inverse_s.append(np.concatenate([high, low], axis=0))
    over_r = np.exp(1j * np.outer(np.arange(RADIX), turn) / (RADIX * SIDE))
    over_r = np.stack([over_r.real, over_r.imag], axis=1)[..., None]
    over_r = np.broadcast_to(over_r, (RADIX, 2, SIDE, LANES)).astype(np.float32)
    q = np.arange(RADIX)[:, None, None]
    over_l = np.exp(1j * side * (turn[:, None] + 256 * np.pi * q) / TOKENS)
    over_l = np.stack([over_l.real, over_l.imag], axis=1).astype(np.float32)
    matrix = np.exp(2j * np.pi * np.outer(side, side) / SIDE)
    form = np.block([[matrix.real, matrix.imag], [-matrix.imag, matrix.real]])
    forward_l = np.stack(two_halves(form))
    inverse_l = np.stack(two_halves(form.T))
    return np.stack(forward_s), np.stack(inverse_s), forward_l, inverse_l, over_r, over_l


def dft4(a, b, c, d, sign):
    t0 = (a[0] + c[0], a[1] + c[1])
    t1 = (a[0] - c[0], a[1] - c[1])
    t2 = (b[0] + d[0], b[1] + d[1])
    t3 = (b[0] - d[0], b[1] - d[1])
    if sign < 0:
        t3 = (-t3[0], -t3[1])
    return [
        (t0[0] + t2[0], t0[1] + t2[1]),
        (t1[0] - t3[1], t1[1] + t3[0]),
        (t0[0] - t2[0], t0[1] - t2[1]),
        (t1[0] + t3[1], t1[1] - t3[0]),
    ]


def dft8(u, sign):
    even = dft4(u[0], u[2], u[4], u[6], sign)
    odd = dft4(u[1], u[3], u[5], u[7], sign)
    half = math.sqrt(0.5)
    turned = [
        odd[0],
        (half * (odd[1][0] - sign * odd[1][1]), half * (odd[1][1] + sign * odd[1][0])),
        (-sign * odd[2][1], sign * odd[2][0]),
        (half * (-odd[3][0] - sign * odd[3][1]), half * (sign * odd[3][0] - odd[3][1])),
    ]
    plus = [(e[0] + o[0], e[1] + o[1]) for e, o in zip(even, turned)]
    minus = [(e[0] - o[0], e[1] - o[1]) for e, o in zip(even, turned)]
    return plus + minus


def split(values):
    high = values.astype(jnp.bfloat16)
    low = (values - high.astype(jnp.float32)).astype(jnp.bfloat16)
    return high, low


def dot(left, right):
    return jnp.dot(left, right, preferred_element_type=jnp.float32)


def dot_from_right(values, table):
    high, low = split(values)
    count = values.shape[0]
    both = dot(jnp.concatenate([high, low], axis=0), table[0])
    return both[:count] + both[count:] + dot(high, table[1])


def times(a, b):
    return a[0] * b[0] - a[1] * b[1], a[0] * b[1] + a[1] * b[0]


def times_conjugate(a, b):
    return a[0] * b[0] + a[1] * b[1], a[1] * b[0] - a[0] * b[1]


def parts(values):
    return values[:, :LANES], values[:, LANES:]


def over_s_forward(blocks_of, count, forward_s, loads, z):
    for r in range(RADIX):
        loads[r].wait()
        samples = [blocks_of(row, r).reshape(SIDE, LANES) for row in range(count)]
        high, low = split(jnp.concatenate(samples, axis=1))
        both = dot(forward_s[r], jnp.concatenate([high, low], axis=0))
        out = both[: 2 * SIDE] + both[2 * SIDE :]
        z[r] = out.reshape(2, SIDE, count * LANES)


def over_r_forward(z, row, span, over_l):
    lanes = pl.ds(row * LANES, LANES)
    u = [(z[r, 0, span, lanes], z[r, 1, span, lanes]) for r in range(RADIX)]
    out = []
    for q, value in enumerate(dft8(u, 1)):
        value = times(value, (over_l[q, 0, span, :], over_l[q, 1, span, :]))
        out.append(jnp.concatenate(value, axis=1))
    return out


def over_r_inverse(values, span, over_l):
    v = []
    for q in range(RADIX):
        value = parts(values[q * STEP : (q + 1) * STEP])
        v.append(times_conjugate(value, (over_l[q, 0, span, :], over_l[q, 1, span, :])))
    return dft8(v, -1)


def over_s_inverse(high, low, table):
    both = dot(table, high)
    return both[:SIDE] + both[SIDE:] + dot(table[:SIDE], low)


def load_each(source, target, sems):
    copies = [pltpu.make_async_copy(source.at[r], target.at[r], sems.at[r]) for r in range(RADIX)]
    for copy in copies:
        copy.start()
    return copies


def filter_kernel(
    rows, forward_s, inverse_s, forward_l, inverse_l, over_r, over_l,
    terms, grads, half, z, back, held, forward_in, sems, load_sems,
):
    loads = load_each(forward_s, forward_in, load_sems)
    half[...] = rows[:, 4 * RADIX :]
    over_s_forward(lambda row, r: rows[:, row * RADIX + r], 4, forward_in, loads, z)
    size = RADIX * STEP
    copies = []
    for step in range(SIDE // STEP):
        span = pl.ds(step * STEP, STEP)
        blocks = []
        for row in range(4):
            blocks += over_r_forward(z, row, span, over_l)
        spectra = dot_from_right(jnp.concatenate(blocks, axis=0), forward_l)
        held[step] = spectra[2 * size :]
        copies.append(pltpu.make_async_copy(held.at[step], grads.at[step], sems.at[step]))
        copies[-1].start()
        first = times_conjugate(parts(spectra[2 * size : 3 * size]), parts(spectra[:size]))
        second = times_conjugate(parts(spectra[3 * size :]), parts(spectra[size : 2 * size]))
        product = jnp.concatenate([first[0] + second[0], first[1] + second[1]], axis=1)
        values = dot_from_right(product, inverse_l)
        for r, value in enumerate(over_r_inverse(values, span, over_l)):
            value = times_conjugate(value, (over_r[r, 0, span, :], over_r[r, 1, span, :]))
            lanes = pl.ds(r * LANES, LANES)
            for part in range(2):
                high, low = split(value[part])
                back[0, part, span, lanes] = high
                back[1, part, span, lanes] = low
    shape = (2 * SIDE, RADIX * LANES)
    out = over_s_inverse(back[0].reshape(shape), back[1].reshape(shape), inverse_s[...])
    for r in range(RADIX):
        value = out[:, r * LANES : (r + 1) * LANES]
        terms[:, r] = value.reshape(terms.shape[0], terms.shape[2], LANES)
    for copy in copies:
        copy.wait()


def input_kernel(
    core, mine, other, grads, forward_s, inverse_s, forward_l, inverse_l, over_l,
    out, z, back, grads_in, forward_in, inverse_in, turns_in, out_held, sems, load_sems,
):
    loads = load_each(forward_s, forward_in, load_sems)
    load_turns = pltpu.make_async_copy(over_l, turns_in, sems.at[0])
    load_grads = pltpu.make_async_copy(grads, grads_in, sems.at[1])
    load_inverse = pltpu.make_async_copy(inverse_s, inverse_in, sems.at[2])
    for copy in (load_turns, load_grads, load_inverse):
        copy.start()
    size = RADIX * STEP
    near = core[0] == 0
    per_half = mine.shape[1]

    def filter_block(row, r):
        own, far = mine[:, r % per_half], other[:, r % per_half]
        return jnp.where(near, own, far) if r < per_half else jnp.where(near, far, own)

    over_s_forward(filter_block, 1, forward_in, loads, z)
    load_turns.wait()
    load_grads.wait()
    for step in range(SIDE // STEP):
        span = pl.ds(step * STEP, STEP)
        spectrum = dot_from_right(
            jnp.concatenate(over_r_forward(z, 0, span, turns_in), axis=0), forward_l
        )
        products = []
        for row in range(2):
            grad = grads_in[step, row * size : (row + 1) * size]
            products.append(
                jnp.concatenate(times_conjugate(parts(grad), parts(spectrum)), axis=1)
            )
        values = dot_from_right(jnp.concatenate(products, axis=0), inverse_l)
        for row in range(2):
            lanes = pl.ds(row * LANES, LANES)
            one = values[row * size : (row + 1) * size]
            for r, value in enumerate(over_r_inverse(one, span, turns_in)):
                for part in range(2):
                    high, low = split(value[part])
                    back[0, r, part, span, lanes] = high
                    back[1, r, part, span, lanes] = low
    shape = (2 * SIDE, 2 * LANES)
    load_inverse.wait()
    copies = []
    for r in range(RADIX):
        samples = over_s_inverse(back[0, r].reshape(shape), back[1, r].reshape(shape), inverse_in[r])
        for row in range(2):
            value = samples[:, row * LANES : (row + 1) * LANES]
            out_held[:, row, r] = value.reshape(out.shape[0], out.shape[3], LANES)
        copies.append(pltpu.make_async_copy(out_held.at[:, :, r], out.at[:, :, r], sems.at[3 + r]))
        copies[-1].start()
    for copy in copies:
        copy.wait()


def in_vmem(count):
    return [pl.BlockSpec(memory_space=pltpu.VMEM)] * count


def in_hbm(count):
    return [pl.BlockSpec(memory_space=pltpu.HBM)] * count


def filter_terms(rows, consts):
    blocks, tiles, part, lanes = rows.shape
    forward_s, inverse_s, forward_l, inverse_l, over_r, over_l = consts
    steps = SIDE // STEP
    grads = (steps, 2 * RADIX * STEP, 2 * LANES)
    return pl.pallas_call(
        filter_kernel,
        out_shape=(
            jax.ShapeDtypeStruct((blocks, RADIX, part, lanes), jnp.float32),
            jax.ShapeDtypeStruct(grads, jnp.float32),
            jax.ShapeDtypeStruct((blocks, tiles - 4 * RADIX, part, lanes), jnp.float32),
        ),
        in_specs=[*in_vmem(1), *in_hbm(1), *in_vmem(5)],
        out_specs=(in_vmem(1)[0], in_hbm(1)[0], in_vmem(1)[0]),
        scratch_shapes=[
            pltpu.VMEM((RADIX, 2, SIDE, 4 * LANES), jnp.float32),
            pltpu.VMEM((2, 2, SIDE, RADIX * LANES), jnp.bfloat16),
            pltpu.VMEM(grads, jnp.float32),
            pltpu.VMEM(forward_s.shape, jnp.bfloat16),
            pltpu.SemaphoreType.DMA((steps,)),
            pltpu.SemaphoreType.DMA((RADIX,)),
        ],
        compiler_params=pltpu.CompilerParams(vmem_limit_bytes=50 << 20),
        cost_estimate=pl.CostEstimate(
            flops=4_000_000_000, bytes_accessed=10_000_000, transcendentals=0
        ),
        name="filter_terms",
    )(rows, forward_s, inverse_s[0], forward_l, inverse_l, over_r, over_l)


def input_rows(core, mine, other, grads, consts):
    blocks, tiles, part, lanes = mine.shape
    forward_s, inverse_s, forward_l, inverse_l, _, over_l = consts
    out = (blocks, 2, RADIX, part, lanes)
    return pl.pallas_call(
        input_kernel,
        out_shape=jax.ShapeDtypeStruct(out, jnp.float32),
        in_specs=[
            pl.BlockSpec(memory_space=pltpu.SMEM),
            *in_vmem(2),
            *in_hbm(3),
            *in_vmem(2),
            *in_hbm(1),
        ],
        out_specs=in_hbm(1)[0],
        scratch_shapes=[
            pltpu.VMEM((RADIX, 2, SIDE, LANES), jnp.float32),
            pltpu.VMEM((2, RADIX, 2, SIDE, 2 * LANES), jnp.bfloat16),
            pltpu.VMEM(grads.shape, jnp.float32),
            pltpu.VMEM(forward_s.shape, jnp.bfloat16),
            pltpu.VMEM(inverse_s.shape, jnp.bfloat16),
            pltpu.VMEM(over_l.shape, jnp.float32),
            pltpu.VMEM(out, jnp.float32),
            pltpu.SemaphoreType.DMA((3 + RADIX,)),
            pltpu.SemaphoreType.DMA((RADIX,)),
        ],
        compiler_params=pltpu.CompilerParams(vmem_limit_bytes=60 << 20),
        cost_estimate=pl.CostEstimate(
            flops=2_500_000_000, bytes_accessed=10_000_000, transcendentals=0
        ),
        name="input_rows",
    )(core, mine, other, grads, forward_s, inverse_s, forward_l, inverse_l, over_l)


def sum_over_chan(value, chan):
    depth = chan // 2

    def moved(array, shift):
        ring = [
            (2 * z + c, 2 * ((z + shift) % depth) + c) for z in range(depth) for c in range(2)
        ]
        return lax.ppermute(array, "chan", ring)

    value = value + lax.ppermute(value, "chan", [(i, i ^ 1) for i in range(chan)])
    if depth != 8:
        total = value
        for shift in range(1, depth):
            total = total + moved(value, shift)
        return total
    below, above = moved(value, 1), moved(value, -1)
    pair = value + above
    triple = pair + below
    return triple + moved(triple, -3) + moved(pair, 3)


def local(saved_input, out_grad, filters):
    batch, channels, tokens = saved_input.shape
    groups = filters.shape[0]
    devices = lax.axis_size("ctx")
    chan = lax.axis_size("chan")
    core = lax.axis_index("chan") % 2
    part = tokens // (RADIX * LANES)
    half = RADIX // 2
    consts = tuple(jnp.asarray(t) for t in tables())
    shape = (batch, channels, part, RADIX, LANES)
    by_channel = [
        v.reshape(shape).transpose(1, 0, 3, 2, 4).reshape(channels, batch * RADIX, part, LANES)
        for v in (saved_input, out_grad)
    ]
    own_filter = filters.reshape(groups, part, 2, half, LANES)
    own_filter = jnp.where(core == 0, own_filter[:, :, 0], own_filter[:, :, 1]).swapaxes(1, 2)
    own_filter = jnp.tile(own_filter, (channels // groups, 1, 1, 1))
    packed = jnp.concatenate([*by_channel, own_filter], axis=1)
    rows = lax.all_to_all(packed, "ctx", 0, 0, tiled=True)
    terms, grads, mine = filter_terms(rows, consts)
    other = lax.ppermute(mine, "chan", [(i, i ^ 1) for i in range(chan)])
    terms = lax.all_to_all(terms, "ctx", 0, 0, tiled=True)
    inputs = input_rows(core.reshape(1), mine, other, grads, consts)
    total = jnp.sum(terms.reshape(devices // groups, groups, RADIX, part, LANES), axis=0)
    inputs, total = lax.optimization_barrier((inputs, total))
    inputs = lax.all_to_all(inputs, "ctx", 0, 0, tiled=True)
    total = sum_over_chan(total, chan)
    per_filter = channels // groups
    norm = float(tokens * devices * batch * per_filter * chan) ** -0.5
    filter_grad = total.swapaxes(1, 2).reshape(groups, tokens) * (norm / TOKENS)
    input_grad = (inputs * (1.0 / TOKENS)).transpose(1, 0, 3, 2, 4)
    return input_grad.reshape(batch, channels, tokens).astype(jnp.bfloat16), filter_grad


def solution(mesh):
    placed = (P(None, "chan", "ctx"), P(None, "chan", "ctx"), P(None, "ctx"))
    return jax.shard_map(
        local,
        mesh=mesh,
        in_specs=placed,
        out_specs=(P(None, "chan", "ctx"), P(None, "ctx")),
        check_vma=False,
    )
```

```python
import functools
import math

import jax
import jax.numpy as jnp
import ml_dtypes
import numpy as np
from jax import lax
from jax.experimental import pallas as pl
from jax.experimental.pallas import tpu as pltpu
from jax.sharding import PartitionSpec as P

RADIX = 8
SIDE = 128
TOKENS = RADIX * SIDE * SIDE
LANES = 128
STEP = 32


def two_halves(matrix):
    high = matrix.astype(ml_dtypes.bfloat16)
    low = (matrix - high.astype(np.float64)).astype(ml_dtypes.bfloat16)
    return high, low


@functools.cache
def tables():
    side = np.arange(SIDE)
    turn = np.pi / 2 + 2 * np.pi * side
    forward_s, inverse_s = [], []
    for r in range(RADIX):
        matrix = np.exp(1j * np.outer(turn, side + r / RADIX) / SIDE)
        high, low = two_halves(np.concatenate([matrix.real, matrix.imag], axis=0))
        forward_s.append(np.concatenate([high, low], axis=0))
        high, low = two_halves(np.concatenate([matrix.real.T, matrix.imag.T], axis=1))
        inverse_s.append(np.concatenate([high, low], axis=0))
    over_r = np.exp(1j * np.outer(np.arange(RADIX), turn) / (RADIX * SIDE))
    over_r = np.stack([over_r.real, over_r.imag], axis=1)[..., None]
    over_r = np.broadcast_to(over_r, (RADIX, 2, SIDE, LANES)).astype(np.float32)
    q = np.arange(RADIX)[:, None, None]
    over_l = np.exp(1j * side * (turn[:, None] + 256 * np.pi * q) / TOKENS)
    over_l = np.stack([over_l.real, over_l.imag], axis=1).astype(np.float32)
    matrix = np.exp(2j * np.pi * np.outer(side, side) / SIDE)
    form = np.block([[matrix.real, matrix.imag], [-matrix.imag, matrix.real]])
    forward_l = np.stack(two_halves(form))
    inverse_l = np.stack(two_halves(form.T))
    return np.stack(forward_s), np.stack(inverse_s), forward_l, inverse_l, over_r, over_l


def dft4(a, b, c, d, sign):
    t0 = (a[0] + c[0], a[1] + c[1])
    t1 = (a[0] - c[0], a[1] - c[1])
    t2 = (b[0] + d[0], b[1] + d[1])
    t3 = (b[0] - d[0], b[1] - d[1])
    if sign < 0:
        t3 = (-t3[0], -t3[1])
    return [
        (t0[0] + t2[0], t0[1] + t2[1]),
        (t1[0] - t3[1], t1[1] + t3[0]),
        (t0[0] - t2[0], t0[1] - t2[1]),
        (t1[0] + t3[1], t1[1] - t3[0]),
    ]


def dft8(u, sign):
    even = dft4(u[0], u[2], u[4], u[6], sign)
    odd = dft4(u[1], u[3], u[5], u[7], sign)
    half = math.sqrt(0.5)
    turned = [
        odd[0],
        (half * (odd[1][0] - sign * odd[1][1]), half * (odd[1][1] + sign * odd[1][0])),
        (-sign * odd[2][1], sign * odd[2][0]),
        (half * (-odd[3][0] - sign * odd[3][1]), half * (sign * odd[3][0] - odd[3][1])),
    ]
    plus = [(e[0] + o[0], e[1] + o[1]) for e, o in zip(even, turned)]
    minus = [(e[0] - o[0], e[1] - o[1]) for e, o in zip(even, turned)]
    return plus + minus


def split(values):
    high = values.astype(jnp.bfloat16)
    low = (values - high.astype(jnp.float32)).astype(jnp.bfloat16)
    return high, low


def dot(left, right):
    return jnp.dot(left, right, preferred_element_type=jnp.float32)


def dot_from_right(values, table):
    high, low = split(values)
    count = values.shape[0]
    both = dot(jnp.concatenate([high, low], axis=0), table[0])
    return both[:count] + both[count:] + dot(high, table[1])


def times(a, b):
    return a[0] * b[0] - a[1] * b[1], a[0] * b[1] + a[1] * b[0]


def times_conjugate(a, b):
    return a[0] * b[0] + a[1] * b[1], a[1] * b[0] - a[0] * b[1]


def parts(values):
    return values[:, :LANES], values[:, LANES:]


def over_s_forward(blocks_of, count, forward_s, z):
    for r in range(RADIX):
        samples = [blocks_of(row, r).reshape(SIDE, LANES) for row in range(count)]
        high, low = split(jnp.concatenate(samples, axis=1))
        first = forward_s[r, : 2 * SIDE]
        second = forward_s[r, 2 * SIDE :]
        table = jnp.concatenate(
            [
                jnp.concatenate([first, first], axis=1),
                jnp.concatenate([second, jnp.zeros_like(second)], axis=1),
            ],
            axis=0,
        )
        both = dot(table, jnp.concatenate([high, low], axis=0))
        out = both[: 2 * SIDE] + both[2 * SIDE :]
        z[r] = out.reshape(2, SIDE, count * LANES)


def over_r_forward(z, row, span, over_l):
    lanes = pl.ds(row * LANES, LANES)
    u = [(z[r, 0, span, lanes], z[r, 1, span, lanes]) for r in range(RADIX)]
    out = []
    for q, value in enumerate(dft8(u, 1)):
        value = times(value, (over_l[q, 0, span, :], over_l[q, 1, span, :]))
        out.append(jnp.concatenate(value, axis=1))
    return out


def over_r_inverse(values, span, over_l):
    v = []
    for q in range(RADIX):
        value = parts(values[q * STEP : (q + 1) * STEP])
        v.append(times_conjugate(value, (over_l[q, 0, span, :], over_l[q, 1, span, :])))
    return dft8(v, -1)


def over_s_inverse(high, low, table):
    both = dot(table, high)
    return both[:SIDE] + both[SIDE:] + dot(table[:SIDE], low)


def filter_kernel(
    rows, forward_s, inverse_s, forward_l, inverse_l, over_r, over_l,
    terms, grads, half, z, back, held, sems,
):
    half[...] = rows[:, 4 * RADIX :]
    over_s_forward(lambda row, r: rows[:, row * RADIX + r], 4, forward_s, z)
    size = RADIX * STEP
    copies = []
    for step in range(SIDE // STEP):
        span = pl.ds(step * STEP, STEP)
        blocks = []
        for row in range(4):
            blocks += over_r_forward(z, row, span, over_l)
        spectra = dot_from_right(jnp.concatenate(blocks, axis=0), forward_l)
        held[step] = spectra[2 * size :]
        copies.append(pltpu.make_async_copy(held.at[step], grads.at[step], sems.at[step]))
        first = times_conjugate(parts(spectra[2 * size : 3 * size]), parts(spectra[:size]))
        second = times_conjugate(parts(spectra[3 * size :]), parts(spectra[size : 2 * size]))
        product = jnp.concatenate([first[0] + second[0], first[1] + second[1]], axis=1)
        values = dot_from_right(product, inverse_l)
        for r, value in enumerate(over_r_inverse(values, span, over_l)):
            value = times_conjugate(value, (over_r[r, 0, span, :], over_r[r, 1, span, :]))
            lanes = pl.ds(r * LANES, LANES)
            for part in range(2):
                high, low = split(value[part])
                back[0, part, span, lanes] = high
                back[1, part, span, lanes] = low
    for copy in copies:
        copy.start()
    shape = (2 * SIDE, RADIX * LANES)
    out = over_s_inverse(back[0].reshape(shape), back[1].reshape(shape), inverse_s[...])
    for r in range(RADIX):
        value = out[:, r * LANES : (r + 1) * LANES]
        terms[:, r] = value.reshape(terms.shape[0], terms.shape[2], LANES)
    for copy in copies:
        copy.wait()


def input_kernel(
    core, mine, other, grads, forward_s, inverse_s, forward_l, inverse_l, over_l,
    out, z, back, grads_in, forward_in, inverse_in, turns_in, out_held, sems,
):
    load_forward = pltpu.make_async_copy(forward_s, forward_in, sems.at[3 + RADIX])
    load_forward.start()
    load_turns = pltpu.make_async_copy(over_l, turns_in, sems.at[0])
    load_grads = pltpu.make_async_copy(grads, grads_in, sems.at[1])
    load_inverse = pltpu.make_async_copy(inverse_s, inverse_in, sems.at[2])
    for copy in (load_turns, load_grads, load_inverse):
        copy.start()
    size = RADIX * STEP
    near = core[0] == 0
    per_half = mine.shape[1]

    def filter_block(row, r):
        own, far = mine[:, r % per_half], other[:, r % per_half]
        return jnp.where(near, own, far) if r < per_half else jnp.where(near, far, own)

    load_forward.wait()
    over_s_forward(filter_block, 1, forward_in, z)
    load_turns.wait()
    load_grads.wait()
    for step in range(SIDE // STEP):
        span = pl.ds(step * STEP, STEP)
        spectrum = dot_from_right(
            jnp.concatenate(over_r_forward(z, 0, span, turns_in), axis=0), forward_l
        )
        products = []
        for row in range(2):
            grad = grads_in[step, row * size : (row + 1) * size]
            products.append(
                jnp.concatenate(times_conjugate(parts(grad), parts(spectrum)), axis=1)
            )
        values = dot_from_right(jnp.concatenate(products, axis=0), inverse_l)
        for row in range(2):
            lanes = pl.ds(row * LANES, LANES)
            one = values[row * size : (row + 1) * size]
            for r, value in enumerate(over_r_inverse(one, span, turns_in)):
                for part in range(2):
                    high, low = split(value[part])
                    back[0, r, part, span, lanes] = high
                    back[1, r, part, span, lanes] = low
    shape = (2 * SIDE, 2 * LANES)
    load_inverse.wait()
    copies = []
    for r in range(RADIX):
        samples = over_s_inverse(back[0, r].reshape(shape), back[1, r].reshape(shape), inverse_in[r])
        for row in range(2):
            value = samples[:, row * LANES : (row + 1) * LANES]
            out_held[:, row, r] = value.reshape(out.shape[0], out.shape[3], LANES)
        copies.append(pltpu.make_async_copy(out_held.at[:, :, r], out.at[:, :, r], sems.at[3 + r]))
        copies[-1].start()
    for copy in copies:
        copy.wait()


def in_vmem(count):
    return [pl.BlockSpec(memory_space=pltpu.VMEM)] * count


def in_hbm(count):
    return [pl.BlockSpec(memory_space=pltpu.HBM)] * count


def filter_terms(rows, consts):
    blocks, tiles, part, lanes = rows.shape
    forward_s, inverse_s, forward_l, inverse_l, over_r, over_l = consts
    steps = SIDE // STEP
    grads = (steps, 2 * RADIX * STEP, 2 * LANES)
    return pl.pallas_call(
        filter_kernel,
        out_shape=(
            jax.ShapeDtypeStruct((blocks, RADIX, part, lanes), jnp.float32),
            jax.ShapeDtypeStruct(grads, jnp.float32),
            jax.ShapeDtypeStruct((blocks, tiles - 4 * RADIX, part, lanes), jnp.float32),
        ),
        in_specs=in_vmem(7),
        out_specs=(in_vmem(1)[0], in_hbm(1)[0], in_vmem(1)[0]),
        scratch_shapes=[
            pltpu.VMEM((RADIX, 2, SIDE, 4 * LANES), jnp.float32),
            pltpu.VMEM((2, 2, SIDE, RADIX * LANES), jnp.bfloat16),
            pltpu.VMEM(grads, jnp.float32),
            pltpu.SemaphoreType.DMA((steps,)),
        ],
        compiler_params=pltpu.CompilerParams(vmem_limit_bytes=48 << 20),
        cost_estimate=pl.CostEstimate(
            flops=4_000_000_000, bytes_accessed=10_000_000, transcendentals=0
        ),
        name="filter_terms",
    )(rows, forward_s, inverse_s[0], forward_l, inverse_l, over_r, over_l)


def input_rows(core, mine, other, grads, consts):
    blocks, tiles, part, lanes = mine.shape
    forward_s, inverse_s, forward_l, inverse_l, _, over_l = consts
    out = (blocks, 2, RADIX, part, lanes)
    return pl.pallas_call(
        input_kernel,
        out_shape=jax.ShapeDtypeStruct(out, jnp.float32),
        in_specs=[
            pl.BlockSpec(memory_space=pltpu.SMEM),
            *in_vmem(2),
            *in_hbm(3),
            *in_vmem(2),
            *in_hbm(1),
        ],
        out_specs=in_hbm(1)[0],
        scratch_shapes=[
            pltpu.VMEM((RADIX, 2, SIDE, LANES), jnp.float32),
            pltpu.VMEM((2, RADIX, 2, SIDE, 2 * LANES), jnp.bfloat16),
            pltpu.VMEM(grads.shape, jnp.float32),
            pltpu.VMEM(forward_s.shape, jnp.bfloat16),
            pltpu.VMEM(inverse_s.shape, jnp.bfloat16),
            pltpu.VMEM(over_l.shape, jnp.float32),
            pltpu.VMEM(out, jnp.float32),
            pltpu.SemaphoreType.DMA((4 + RADIX,)),
        ],
        compiler_params=pltpu.CompilerParams(vmem_limit_bytes=60 << 20),
        cost_estimate=pl.CostEstimate(
            flops=2_500_000_000, bytes_accessed=10_000_000, transcendentals=0
        ),
        name="input_rows",
    )(core, mine, other, grads, forward_s, inverse_s, forward_l, inverse_l, over_l)


def sum_over_chan(value, chan):
    depth = chan // 2

    def moved(array, shift, swap=False):
        ring = []
        for z in range(depth):
            ring.append((2 * z, 2 * ((z + shift) % depth) + swap))
            ring.append((2 * z + 1, 2 * ((z - shift) % depth) + 1 - swap))
        return lax.ppermute(array, "chan", ring)

    value = value + moved(value, 0, True)
    if depth < 2 or depth & (depth - 1):
        total = value
        for shift in range(1, depth):
            total = total + moved(value, shift)
        return total
    reach = 1
    while 2 * reach < depth:
        value = value + moved(value, reach)
        reach *= 2
    return value + moved(value, 1, True)


def local(saved_input, out_grad, filters):
    batch, channels, tokens = saved_input.shape
    groups = filters.shape[0]
    devices = lax.axis_size("ctx")
    chan = lax.axis_size("chan")
    core = lax.axis_index("chan") % 2
    part = tokens // (RADIX * LANES)
    half = RADIX // 2
    consts = tuple(jnp.asarray(t) for t in tables())
    shape = (batch, channels, part, RADIX, LANES)
    by_channel = [
        v.reshape(shape).transpose(1, 0, 3, 2, 4).reshape(channels, batch * RADIX, part, LANES)
        for v in (saved_input, out_grad)
    ]
    own_filter = filters.reshape(groups, part, 2, half, LANES)
    own_filter = jnp.where(core == 0, own_filter[:, :, 0], own_filter[:, :, 1]).swapaxes(1, 2)
    own_filter = jnp.tile(own_filter, (channels // groups, 1, 1, 1))
    packed = jnp.concatenate([*by_channel, own_filter], axis=1)
    rows = lax.all_to_all(packed, "ctx", 0, 0, tiled=True)
    terms, grads, mine = filter_terms(rows, consts)
    other = lax.ppermute(mine, "chan", [(i, i ^ 1) for i in range(chan)])
    terms = lax.all_to_all(terms, "ctx", 0, 0, tiled=True)
    inputs = input_rows(core.reshape(1), mine, other, grads, consts)
    total = jnp.sum(terms.reshape(devices // groups, groups, RADIX, part, LANES), axis=0)
    inputs, total = lax.optimization_barrier((inputs, total))
    inputs = lax.all_to_all(inputs, "ctx", 0, 0, tiled=True)
    total = sum_over_chan(total, chan)
    per_filter = channels // groups
    norm = float(tokens * devices * batch * per_filter * chan) ** -0.5
    filter_grad = total.swapaxes(1, 2).reshape(groups, tokens) * (norm / TOKENS)
    input_grad = (inputs * (1.0 / TOKENS)).transpose(1, 0, 3, 2, 4)
    return input_grad.reshape(batch, channels, tokens).astype(jnp.bfloat16), filter_grad


def solution(mesh):
    placed = (P(None, "chan", "ctx"), P(None, "chan", "ctx"), P(None, "ctx"))
    return jax.shard_map(
        local,
        mesh=mesh,
        in_specs=placed,
        out_specs=(P(None, "chan", "ctx"), P(None, "ctx")),
        check_vma=False,
    )
```

```python
import functools
import math

import jax
import jax.numpy as jnp
import ml_dtypes
import numpy as np
from jax import lax
from jax.experimental import pallas as pl
from jax.experimental.pallas import tpu as pltpu
from jax.sharding import PartitionSpec as P

RADIX = 8
SIDE = 128
TOKENS = RADIX * SIDE * SIDE
LANES = 128
STEP = 32


def two_halves(matrix):
    high = matrix.astype(ml_dtypes.bfloat16)
    low = (matrix - high.astype(np.float64)).astype(ml_dtypes.bfloat16)
    return high, low


@functools.cache
def tables():
    side = np.arange(SIDE)
    turn = np.pi / 2 + 2 * np.pi * side
    forward_s, inverse_s = [], []
    for r in range(RADIX):
        matrix = np.exp(1j * np.outer(turn, side + r / RADIX) / SIDE)
        high, low = two_halves(np.concatenate([matrix.real, matrix.imag], axis=0))
        forward_s.append(np.concatenate([high, low], axis=0))
        high, low = two_halves(np.concatenate([matrix.real.T, matrix.imag.T], axis=1))
        inverse_s.append(np.concatenate([high, low], axis=0))
    over_r = np.exp(1j * np.outer(np.arange(RADIX), turn) / (RADIX * SIDE))
    over_r = np.stack([over_r.real, over_r.imag], axis=1)[..., None]
    over_r = np.broadcast_to(over_r, (RADIX, 2, SIDE, LANES)).astype(np.float32)
    q = np.arange(RADIX)[:, None, None]
    over_l = np.exp(1j * side * (turn[:, None] + 256 * np.pi * q) / TOKENS)
    over_l = np.stack([over_l.real, over_l.imag], axis=1).astype(np.float32)
    matrix = np.exp(2j * np.pi * np.outer(side, side) / SIDE)
    form = np.block([[matrix.real, matrix.imag], [-matrix.imag, matrix.real]])
    forward_l = np.stack(two_halves(form))
    inverse_l = np.stack(two_halves(form.T))
    return np.stack(forward_s), np.stack(inverse_s), forward_l, inverse_l, over_r, over_l


def dft4(a, b, c, d, sign):
    t0 = (a[0] + c[0], a[1] + c[1])
    t1 = (a[0] - c[0], a[1] - c[1])
    t2 = (b[0] + d[0], b[1] + d[1])
    t3 = (b[0] - d[0], b[1] - d[1])
    if sign < 0:
        t3 = (-t3[0], -t3[1])
    return [
        (t0[0] + t2[0], t0[1] + t2[1]),
        (t1[0] - t3[1], t1[1] + t3[0]),
        (t0[0] - t2[0], t0[1] - t2[1]),
        (t1[0] + t3[1], t1[1] - t3[0]),
    ]


def dft8(u, sign):
    even = dft4(u[0], u[2], u[4], u[6], sign)
    odd = dft4(u[1], u[3], u[5], u[7], sign)
    half = math.sqrt(0.5)
    turned = [
        odd[0],
        (half * (odd[1][0] - sign * odd[1][1]), half * (odd[1][1] + sign * odd[1][0])),
        (-sign * odd[2][1], sign * odd[2][0]),
        (half * (-odd[3][0] - sign * odd[3][1]), half * (sign * odd[3][0] - odd[3][1])),
    ]
    plus = [(e[0] + o[0], e[1] + o[1]) for e, o in zip(even, turned)]
    minus = [(e[0] - o[0], e[1] - o[1]) for e, o in zip(even, turned)]
    return plus + minus


def split(values):
    high = values.astype(jnp.bfloat16)
    low = (values - high.astype(jnp.float32)).astype(jnp.bfloat16)
    return high, low


def dot(left, right):
    return jnp.dot(left, right, preferred_element_type=jnp.float32)


def dot_from_right(values, table):
    high, low = split(values)
    count = values.shape[0]
    both = dot(jnp.concatenate([high, low], axis=0), table[0])
    return both[:count] + both[count:] + dot(high, table[1])


def times(a, b):
    return a[0] * b[0] - a[1] * b[1], a[0] * b[1] + a[1] * b[0]


def times_conjugate(a, b):
    return a[0] * b[0] + a[1] * b[1], a[1] * b[0] - a[0] * b[1]


def parts(values):
    return values[:, :LANES], values[:, LANES:]


def over_s_forward(blocks_of, count, forward_s, z):
    for r in range(RADIX):
        samples = [blocks_of(row, r).reshape(SIDE, LANES) for row in range(count)]
        high, low = split(jnp.concatenate(samples, axis=1))
        first = forward_s[r, : 2 * SIDE]
        second = forward_s[r, 2 * SIDE :]
        table = jnp.concatenate(
            [
                jnp.concatenate([first, first], axis=1),
                jnp.concatenate([second, jnp.zeros_like(second)], axis=1),
            ],
            axis=0,
        )
        both = dot(table, jnp.concatenate([high, low], axis=0))
        out = both[: 2 * SIDE] + both[2 * SIDE :]
        z[r] = out.reshape(2, SIDE, count * LANES)


def over_r_forward(z, row, span, over_l):
    lanes = pl.ds(row * LANES, LANES)
    u = [(z[r, 0, span, lanes], z[r, 1, span, lanes]) for r in range(RADIX)]
    out = []
    for q, value in enumerate(dft8(u, 1)):
        value = times(value, (over_l[q, 0, span, :], over_l[q, 1, span, :]))
        out.append(jnp.concatenate(value, axis=1))
    return out


def over_r_inverse(values, span, over_l):
    v = []
    for q in range(RADIX):
        value = parts(values[q * STEP : (q + 1) * STEP])
        v.append(times_conjugate(value, (over_l[q, 0, span, :], over_l[q, 1, span, :])))
    return dft8(v, -1)


def over_s_inverse(high, low, table):
    both = dot(table, high)
    return both[:SIDE] + both[SIDE:] + dot(table[:SIDE], low)


def place(step, row, part):
    tiles = RADIX * STEP // 8
    block, first = divmod(((step * 2 + part) * 2 + row) * tiles, 4 * RADIX)
    return block, pl.ds(first, tiles)


def filter_kernel(
    rows, forward_s, inverse_s, forward_l, inverse_l, over_r, over_l,
    terms, kept, half, z, back,
):
    own_half = rows[:, 4 * RADIX :]
    half[...] = own_half
    kept[:, 4 * RADIX :] = own_half
    over_s_forward(lambda row, r: rows[:, row * RADIX + r], 4, forward_s, z)
    size = RADIX * STEP
    for step in range(SIDE // STEP):
        span = pl.ds(step * STEP, STEP)
        blocks = []
        for row in range(4):
            blocks += over_r_forward(z, row, span, over_l)
        spectra = dot_from_right(jnp.concatenate(blocks, axis=0), forward_l)
        for row in range(2):
            for part, value in enumerate(parts(spectra[(2 + row) * size : (3 + row) * size])):
                kept[place(step, row, part)] = value.reshape(size // 8, 8, LANES)
        first = times_conjugate(parts(spectra[2 * size : 3 * size]), parts(spectra[:size]))
        second = times_conjugate(parts(spectra[3 * size :]), parts(spectra[size : 2 * size]))
        product = jnp.concatenate([first[0] + second[0], first[1] + second[1]], axis=1)
        values = dot_from_right(product, inverse_l)
        for r, value in enumerate(over_r_inverse(values, span, over_l)):
            value = times_conjugate(value, (over_r[r, 0, span, :], over_r[r, 1, span, :]))
            lanes = pl.ds(r * LANES, LANES)
            for part in range(2):
                high, low = split(value[part])
                back[0, part, span, lanes] = high
                back[1, part, span, lanes] = low
    shape = (2 * SIDE, RADIX * LANES)
    out = over_s_inverse(back[0].reshape(shape), back[1].reshape(shape), inverse_s[...])
    for r in range(RADIX):
        value = out[:, r * LANES : (r + 1) * LANES]
        terms[:, r] = value.reshape(terms.shape[0], terms.shape[2], LANES)


def input_kernel(
    core, kept, other, forward_s, inverse_s, forward_l, inverse_l, over_l,
    out, z, back, forward_in, inverse_in, turns_in, out_held, sems,
):
    load_forward = pltpu.make_async_copy(forward_s, forward_in, sems.at[2 + RADIX])
    load_forward.start()
    load_turns = pltpu.make_async_copy(over_l, turns_in, sems.at[0])
    load_inverse = pltpu.make_async_copy(inverse_s, inverse_in, sems.at[1])
    for copy in (load_turns, load_inverse):
        copy.start()
    size = RADIX * STEP
    near = core[0] == 0
    per_half = other.shape[1]

    def filter_block(row, r):
        own, far = kept[:, 4 * RADIX + r % per_half], other[:, r % per_half]
        return jnp.where(near, own, far) if r < per_half else jnp.where(near, far, own)

    load_forward.wait()
    over_s_forward(filter_block, 1, forward_in, z)
    load_turns.wait()
    for step in range(SIDE // STEP):
        span = pl.ds(step * STEP, STEP)
        spectrum = dot_from_right(
            jnp.concatenate(over_r_forward(z, 0, span, turns_in), axis=0), forward_l
        )
        products = []
        for row in range(2):
            grad = [kept[place(step, row, part)].reshape(size, LANES) for part in range(2)]
            products.append(jnp.concatenate(times_conjugate(grad, parts(spectrum)), axis=1))
        values = dot_from_right(jnp.concatenate(products, axis=0), inverse_l)
        for row in range(2):
            lanes = pl.ds(row * LANES, LANES)
            one = values[row * size : (row + 1) * size]
            for r, value in enumerate(over_r_inverse(one, span, turns_in)):
                for part in range(2):
                    high, low = split(value[part])
                    back[0, r, part, span, lanes] = high
                    back[1, r, part, span, lanes] = low
    shape = (2 * SIDE, 2 * LANES)
    load_inverse.wait()
    copies = []
    for r in range(RADIX):
        samples = over_s_inverse(back[0, r].reshape(shape), back[1, r].reshape(shape), inverse_in[r])
        for row in range(2):
            value = samples[:, row * LANES : (row + 1) * LANES]
            out_held[:, row, r] = value.reshape(out.shape[0], out.shape[3], LANES)
        copies.append(pltpu.make_async_copy(out_held.at[:, :, r], out.at[:, :, r], sems.at[2 + r]))
        copies[-1].start()
    for copy in copies:
        copy.wait()


def in_vmem(count):
    return [pl.BlockSpec(memory_space=pltpu.VMEM)] * count


def in_hbm(count):
    return [pl.BlockSpec(memory_space=pltpu.HBM)] * count


def filter_terms(rows, consts):
    blocks, tiles, part, lanes = rows.shape
    forward_s, inverse_s, forward_l, inverse_l, over_r, over_l = consts
    return pl.pallas_call(
        filter_kernel,
        out_shape=(
            jax.ShapeDtypeStruct((blocks, RADIX, part, lanes), jnp.float32),
            jax.ShapeDtypeStruct(rows.shape, jnp.float32),
            jax.ShapeDtypeStruct((blocks, tiles - 4 * RADIX, part, lanes), jnp.float32),
        ),
        in_specs=in_vmem(7),
        out_specs=tuple(in_vmem(3)),
        input_output_aliases={0: 1},
        scratch_shapes=[
            pltpu.VMEM((RADIX, 2, SIDE, 4 * LANES), jnp.float32),
            pltpu.VMEM((2, 2, SIDE, RADIX * LANES), jnp.bfloat16),
        ],
        compiler_params=pltpu.CompilerParams(vmem_limit_bytes=20 << 20),
        cost_estimate=pl.CostEstimate(
            flops=4_000_000_000, bytes_accessed=10_000_000, transcendentals=0
        ),
        name="filter_terms",
    )(rows, forward_s, inverse_s[0], forward_l, inverse_l, over_r, over_l)


def input_rows(core, kept, other, consts):
    blocks, tiles, part, lanes = kept.shape
    forward_s, inverse_s, forward_l, inverse_l, _, over_l = consts
    out = (blocks, 2, RADIX, part, lanes)
    return pl.pallas_call(
        input_kernel,
        out_shape=jax.ShapeDtypeStruct(out, jnp.float32),
        in_specs=[
            pl.BlockSpec(memory_space=pltpu.SMEM),
            *in_vmem(2),
            *in_hbm(2),
            *in_vmem(2),
            *in_hbm(1),
        ],
        out_specs=in_hbm(1)[0],
        scratch_shapes=[
            pltpu.VMEM((RADIX, 2, SIDE, LANES), jnp.float32),
            pltpu.VMEM((2, RADIX, 2, SIDE, 2 * LANES), jnp.bfloat16),
            pltpu.VMEM(forward_s.shape, jnp.bfloat16),
            pltpu.VMEM(inverse_s.shape, jnp.bfloat16),
            pltpu.VMEM(over_l.shape, jnp.float32),
            pltpu.VMEM(out, jnp.float32),
            pltpu.SemaphoreType.DMA((3 + RADIX,)),
        ],
        compiler_params=pltpu.CompilerParams(vmem_limit_bytes=60 << 20),
        cost_estimate=pl.CostEstimate(
            flops=2_500_000_000, bytes_accessed=10_000_000, transcendentals=0
        ),
        name="input_rows",
    )(core, kept, other, forward_s, inverse_s, forward_l, inverse_l, over_l)


def sum_over_chan(value, chan):
    depth = chan // 2

    def moved(array, shift, swap=False):
        ring = []
        for z in range(depth):
            ring.append((2 * z, 2 * ((z + shift) % depth) + swap))
            ring.append((2 * z + 1, 2 * ((z - shift) % depth) + 1 - swap))
        return lax.ppermute(array, "chan", ring)

    value = value + moved(value, 0, True)
    if depth < 2 or depth & (depth - 1):
        total = value
        for shift in range(1, depth):
            total = total + moved(value, shift)
        return total, jnp.zeros_like(total)
    reach = 1
    while 2 * reach < depth:
        value = value + moved(value, reach)
        reach *= 2
    return value, moved(value, 1, True)


def local(saved_input, out_grad, filters):
    batch, channels, tokens = saved_input.shape
    groups = filters.shape[0]
    devices = lax.axis_size("ctx")
    chan = lax.axis_size("chan")
    core = lax.axis_index("chan") % 2
    part = tokens // (RADIX * LANES)
    half = RADIX // 2
    consts = tuple(jnp.asarray(t) for t in tables())
    shape = (batch, channels, part, RADIX, LANES)
    by_channel = [
        v.reshape(shape).transpose(1, 0, 3, 2, 4).reshape(channels, batch * RADIX, part, LANES)
        for v in (saved_input, out_grad)
    ]
    own_filter = filters.reshape(groups, part, 2, half, LANES)
    own_filter = jnp.where(core == 0, own_filter[:, :, 0], own_filter[:, :, 1]).swapaxes(1, 2)
    own_filter = jnp.tile(own_filter, (channels // groups, 1, 1, 1))
    packed = jnp.concatenate([*by_channel, own_filter], axis=1)
    rows = lax.all_to_all(packed, "ctx", 0, 0, tiled=True)
    terms, kept, mine = filter_terms(rows, consts)
    other = lax.ppermute(mine, "chan", [(i, i ^ 1) for i in range(chan)])
    terms = lax.all_to_all(terms, "ctx", 0, 0, tiled=True)
    inputs = input_rows(core.reshape(1), kept, other, consts)
    total = jnp.sum(terms.reshape(devices // groups, groups, RADIX, part, LANES), axis=0)
    inputs, total = lax.optimization_barrier((inputs, total))
    inputs = lax.all_to_all(inputs, "ctx", 0, 0, tiled=True)
    inputs = (inputs * (1.0 / TOKENS)).transpose(1, 0, 3, 2, 4)
    input_grad = inputs.reshape(batch, channels, tokens).astype(jnp.bfloat16)
    total, last = sum_over_chan(total, chan)
    input_grad, last = lax.optimization_barrier((input_grad, last))
    total = total + last
    per_filter = channels // groups
    norm = float(tokens * devices * batch * per_filter * chan) ** -0.5
    filter_grad = total.swapaxes(1, 2).reshape(groups, tokens) * (norm / TOKENS)
    return input_grad, filter_grad


def solution(mesh):
    placed = (P(None, "chan", "ctx"), P(None, "chan", "ctx"), P(None, "ctx"))
    return jax.shard_map(
        local,
        mesh=mesh,
        in_specs=placed,
        out_specs=(P(None, "chan", "ctx"), P(None, "ctx")),
        check_vma=False,
    )
```

```python
import functools
import math

import jax
import jax.numpy as jnp
import ml_dtypes
import numpy as np
from jax import lax
from jax.experimental import pallas as pl
from jax.experimental.pallas import tpu as pltpu
from jax.sharding import PartitionSpec as P

RADIX = 8
SIDE = 128
TOKENS = RADIX * SIDE * SIDE
LANES = 128
STEP = 32


def two_halves(matrix):
    high = matrix.astype(ml_dtypes.bfloat16)
    low = (matrix - high.astype(np.float64)).astype(ml_dtypes.bfloat16)
    return high, low


@functools.cache
def tables():
    side = np.arange(SIDE)
    turn = np.pi / 2 + 2 * np.pi * side
    forward_s, inverse_s = [], []
    for r in range(RADIX):
        matrix = np.exp(1j * np.outer(turn, side + r / RADIX) / SIDE)
        high, low = two_halves(np.concatenate([matrix.real, matrix.imag], axis=0))
        forward_s.append(np.concatenate([high, low], axis=0))
        high, low = two_halves(np.concatenate([matrix.real.T, matrix.imag.T], axis=1))
        inverse_s.append(np.concatenate([high, low], axis=0))
    over_r = np.exp(1j * np.outer(np.arange(RADIX), turn) / (RADIX * SIDE))
    over_r = np.stack([over_r.real, over_r.imag], axis=1)[..., None]
    over_r = np.broadcast_to(over_r, (RADIX, 2, SIDE, LANES)).astype(np.float32)
    q = np.arange(RADIX)[:, None, None]
    over_l = np.exp(1j * side * (turn[:, None] + 256 * np.pi * q) / TOKENS)
    over_l = np.stack([over_l.real, over_l.imag], axis=1).astype(np.float32)
    matrix = np.exp(2j * np.pi * np.outer(side, side) / SIDE)
    form = np.block([[matrix.real, matrix.imag], [-matrix.imag, matrix.real]])
    forward_l = np.stack(two_halves(form))
    inverse_l = np.stack(two_halves(form.T))
    return np.stack(forward_s), np.stack(inverse_s), forward_l, inverse_l, over_r, over_l


def dft4(a, b, c, d, sign):
    t0 = (a[0] + c[0], a[1] + c[1])
    t1 = (a[0] - c[0], a[1] - c[1])
    t2 = (b[0] + d[0], b[1] + d[1])
    t3 = (b[0] - d[0], b[1] - d[1])
    if sign < 0:
        t3 = (-t3[0], -t3[1])
    return [
        (t0[0] + t2[0], t0[1] + t2[1]),
        (t1[0] - t3[1], t1[1] + t3[0]),
        (t0[0] - t2[0], t0[1] - t2[1]),
        (t1[0] + t3[1], t1[1] - t3[0]),
    ]


def dft8(u, sign):
    even = dft4(u[0], u[2], u[4], u[6], sign)
    odd = dft4(u[1], u[3], u[5], u[7], sign)
    half = math.sqrt(0.5)
    turned = [
        odd[0],
        (half * (odd[1][0] - sign * odd[1][1]), half * (odd[1][1] + sign * odd[1][0])),
        (-sign * odd[2][1], sign * odd[2][0]),
        (half * (-odd[3][0] - sign * odd[3][1]), half * (sign * odd[3][0] - odd[3][1])),
    ]
    plus = [(e[0] + o[0], e[1] + o[1]) for e, o in zip(even, turned)]
    minus = [(e[0] - o[0], e[1] - o[1]) for e, o in zip(even, turned)]
    return plus + minus


def split(values):
    high = values.astype(jnp.bfloat16)
    low = (values - high.astype(jnp.float32)).astype(jnp.bfloat16)
    return high, low


def dot(left, right):
    return jnp.dot(left, right, preferred_element_type=jnp.float32)


def dot_from_right(values, table):
    high, low = split(values)
    count = values.shape[0]
    both = dot(jnp.concatenate([high, low], axis=0), table[0])
    return both[:count] + both[count:] + dot(high, table[1])


def times(a, b):
    return a[0] * b[0] - a[1] * b[1], a[0] * b[1] + a[1] * b[0]


def times_conjugate(a, b):
    return a[0] * b[0] + a[1] * b[1], a[1] * b[0] - a[0] * b[1]


def parts(values):
    return values[:, :LANES], values[:, LANES:]


def over_s_forward(blocks_of, count, forward_s, z):
    for r in range(RADIX):
        samples = [blocks_of(row, r).reshape(SIDE, LANES) for row in range(count)]
        high, low = split(jnp.concatenate(samples, axis=1))
        first = forward_s[r, : 2 * SIDE]
        second = forward_s[r, 2 * SIDE :]
        table = jnp.concatenate(
            [
                jnp.concatenate([first, first], axis=1),
                jnp.concatenate([second, jnp.zeros_like(second)], axis=1),
            ],
            axis=0,
        )
        both = dot(table, jnp.concatenate([high, low], axis=0))
        out = both[: 2 * SIDE] + both[2 * SIDE :]
        z[r] = out.reshape(2, SIDE, count * LANES)


def over_r_forward(z, row, span, over_l):
    lanes = pl.ds(row * LANES, LANES)
    u = [(z[r, 0, span, lanes], z[r, 1, span, lanes]) for r in range(RADIX)]
    out = []
    for q, value in enumerate(dft8(u, 1)):
        value = times(value, (over_l[q, 0, span, :], over_l[q, 1, span, :]))
        out.append(jnp.concatenate(value, axis=1))
    return out


def over_r_inverse(values, span, over_l):
    v = []
    for q in range(RADIX):
        value = parts(values[q * STEP : (q + 1) * STEP])
        v.append(times_conjugate(value, (over_l[q, 0, span, :], over_l[q, 1, span, :])))
    return dft8(v, -1)


def over_s_inverse(high, low, table):
    both = dot(table, high)
    return both[:SIDE] + both[SIDE:] + dot(table[:SIDE], low)


def filter_kernel(
    rows, forward_s, inverse_s, forward_l, inverse_l, over_r, over_l,
    terms, grads, half, z, back, held, sems,
):
    half[...] = rows[:, 4 * RADIX :]
    over_s_forward(lambda row, r: rows[:, row * RADIX + r], 4, forward_s, z)
    size = RADIX * STEP
    copies = []
    for step in range(SIDE // STEP):
        span = pl.ds(step * STEP, STEP)
        blocks = []
        for row in range(4):
            blocks += over_r_forward(z, row, span, over_l)
        spectra = dot_from_right(jnp.concatenate(blocks, axis=0), forward_l)
        held[step] = spectra[2 * size :]
        copies.append(pltpu.make_async_copy(held.at[step], grads.at[step], sems.at[step]))
        first = times_conjugate(parts(spectra[2 * size : 3 * size]), parts(spectra[:size]))
        second = times_conjugate(parts(spectra[3 * size :]), parts(spectra[size : 2 * size]))
        product = jnp.concatenate([first[0] + second[0], first[1] + second[1]], axis=1)
        values = dot_from_right(product, inverse_l)
        for r, value in enumerate(over_r_inverse(values, span, over_l)):
            value = times_conjugate(value, (over_r[r, 0, span, :], over_r[r, 1, span, :]))
            lanes = pl.ds(r * LANES, LANES)
            for part in range(2):
                high, low = split(value[part])
                back[0, part, span, lanes] = high
                back[1, part, span, lanes] = low
    for copy in copies:
        copy.start()
    shape = (2 * SIDE, RADIX * LANES)
    out = over_s_inverse(back[0].reshape(shape), back[1].reshape(shape), inverse_s[...])
    for r in range(RADIX):
        value = out[:, r * LANES : (r + 1) * LANES]
        terms[:, r] = value.reshape(terms.shape[0], terms.shape[2], LANES)
    for copy in copies:
        copy.wait()


def input_kernel(
    core, mine, other, grads, forward_s, inverse_s, forward_l, inverse_l, over_l,
    out, z, back, grads_in, forward_in, inverse_in, turns_in, out_held, sems,
):
    load_forward = pltpu.make_async_copy(forward_s, forward_in, sems.at[3 + RADIX])
    load_forward.start()
    load_turns = pltpu.make_async_copy(over_l, turns_in, sems.at[0])
    load_grads = pltpu.make_async_copy(grads, grads_in, sems.at[1])
    load_inverse = pltpu.make_async_copy(inverse_s, inverse_in, sems.at[2])
    for copy in (load_turns, load_grads, load_inverse):
        copy.start()
    size = RADIX * STEP
    near = core[0] == 0
    per_half = mine.shape[1]

    def filter_block(row, r):
        own, far = mine[:, r % per_half], other[:, r % per_half]
        return jnp.where(near, own, far) if r < per_half else jnp.where(near, far, own)

    load_forward.wait()
    over_s_forward(filter_block, 1, forward_in, z)
    load_turns.wait()
    load_grads.wait()
    for step in range(SIDE // STEP):
        span = pl.ds(step * STEP, STEP)
        spectrum = dot_from_right(
            jnp.concatenate(over_r_forward(z, 0, span, turns_in), axis=0), forward_l
        )
        products = []
        for row in range(2):
            grad = grads_in[step, row * size : (row + 1) * size]
            products.append(
                jnp.concatenate(times_conjugate(parts(grad), parts(spectrum)), axis=1)
            )
        values = dot_from_right(jnp.concatenate(products, axis=0), inverse_l)
        for row in range(2):
            lanes = pl.ds(row * LANES, LANES)
            one = values[row * size : (row + 1) * size]
            for r, value in enumerate(over_r_inverse(one, span, turns_in)):
                for part in range(2):
                    high, low = split(value[part])
                    back[0, r, part, span, lanes] = high
                    back[1, r, part, span, lanes] = low
    shape = (2 * SIDE, 2 * LANES)
    load_inverse.wait()
    copies = []
    for r in range(RADIX):
        samples = over_s_inverse(back[0, r].reshape(shape), back[1, r].reshape(shape), inverse_in[r])
        for row in range(2):
            value = samples[:, row * LANES : (row + 1) * LANES]
            out_held[:, row, r] = value.reshape(out.shape[0], out.shape[3], LANES)
        copies.append(pltpu.make_async_copy(out_held.at[:, :, r], out.at[:, :, r], sems.at[3 + r]))
        copies[-1].start()
    for copy in copies:
        copy.wait()


def in_vmem(count):
    return [pl.BlockSpec(memory_space=pltpu.VMEM)] * count


def in_hbm(count):
    return [pl.BlockSpec(memory_space=pltpu.HBM)] * count


def layout_kernel(core, saved_input, out_grad, filters, out, samples, filter_in, sems):
    batch, channels, tokens = saved_input.shape
    groups = filters.shape[0]
    per_half = RADIX // 2
    loads = []
    for array, source in enumerate((saved_input, out_grad)):
        for b in range(batch):
            slot = array * batch + b
            loads.append(pltpu.make_async_copy(source.at[b], samples.at[slot], sems.at[slot]))
    load_filter = pltpu.make_async_copy(filters, filter_in, sems.at[2 * batch])
    for copy in [load_filter, *loads]:
        copy.start()
    load_filter.wait()
    for group in range(groups):
        for r in range(per_half):
            for s in range(tokens // (RADIX * LANES)):
                start = pl.multiple_of((s * RADIX + core[0] * per_half + r) * LANES, LANES)
                row = filter_in[pl.ds(group, 1), pl.ds(start, LANES)]
                out[group, 2 * batch * RADIX + r, pl.ds(s, 1), :] = row
    for channel in range(groups, channels):
        out[channel, 2 * batch * RADIX :] = out[channel % groups, 2 * batch * RADIX :]
    for slot, load in enumerate(loads):
        load.wait()
        for first in range(0, channels, 8):
            for r in range(RADIX):
                for s in range(tokens // (RADIX * LANES)):
                    value = samples[slot, pl.ds(first, 8), pl.ds((s * RADIX + r) * LANES, LANES)]
                    out[pl.ds(first, 8), slot * RADIX + r, s, :] = value


def laid_out(core, saved_input, out_grad, filters):
    arrays = (saved_input, out_grad, filters)
    batch, channels, tokens = saved_input.shape
    part = tokens // (RADIX * LANES)
    tiles = 2 * batch * RADIX + RADIX // 2
    return pl.pallas_call(
        layout_kernel,
        out_shape=jax.ShapeDtypeStruct((channels, tiles, part, LANES), jnp.float32),
        in_specs=[pl.BlockSpec(memory_space=pltpu.SMEM), *in_hbm(3)],
        out_specs=in_vmem(1)[0],
        scratch_shapes=[
            pltpu.VMEM((2 * batch, channels, tokens), jnp.float32),
            pltpu.VMEM(filters.shape, jnp.float32),
            pltpu.SemaphoreType.DMA((2 * batch + 1,)),
        ],
        compiler_params=pltpu.CompilerParams(vmem_limit_bytes=40 << 20),
        name="laid_out",
    )(core, *(pltpu.with_memory_space_constraint(v, pltpu.HBM) for v in arrays))


def filter_terms(rows, consts):
    blocks, tiles, part, lanes = rows.shape
    forward_s, inverse_s, forward_l, inverse_l, over_r, over_l = consts
    steps = SIDE // STEP
    grads = (steps, 2 * RADIX * STEP, 2 * LANES)
    return pl.pallas_call(
        filter_kernel,
        out_shape=(
            jax.ShapeDtypeStruct((blocks, RADIX, part, lanes), jnp.float32),
            pltpu.HBM(grads, jnp.float32),
            jax.ShapeDtypeStruct((blocks, tiles - 4 * RADIX, part, lanes), jnp.float32),
        ),
        in_specs=in_vmem(7),
        out_specs=(in_vmem(1)[0], in_hbm(1)[0], in_vmem(1)[0]),
        scratch_shapes=[
            pltpu.VMEM((RADIX, 2, SIDE, 4 * LANES), jnp.float32),
            pltpu.VMEM((2, 2, SIDE, RADIX * LANES), jnp.bfloat16),
            pltpu.VMEM(grads, jnp.float32),
            pltpu.SemaphoreType.DMA((steps,)),
        ],
        compiler_params=pltpu.CompilerParams(vmem_limit_bytes=20 << 20),
        cost_estimate=pl.CostEstimate(
            flops=4_000_000_000, bytes_accessed=10_000_000, transcendentals=0
        ),
        name="filter_terms",
    )(rows, forward_s, inverse_s[0], forward_l, inverse_l, over_r, over_l)


def input_rows(core, mine, other, grads, consts):
    blocks, tiles, part, lanes = mine.shape
    forward_s, inverse_s, forward_l, inverse_l, _, over_l = consts
    out = (blocks, 2, RADIX, part, lanes)
    return pl.pallas_call(
        input_kernel,
        out_shape=jax.ShapeDtypeStruct(out, jnp.float32),
        in_specs=[
            pl.BlockSpec(memory_space=pltpu.SMEM),
            *in_vmem(2),
            *in_hbm(3),
            *in_vmem(2),
            *in_hbm(1),
        ],
        out_specs=in_hbm(1)[0],
        scratch_shapes=[
            pltpu.VMEM((RADIX, 2, SIDE, LANES), jnp.float32),
            pltpu.VMEM((2, RADIX, 2, SIDE, 2 * LANES), jnp.bfloat16),
            pltpu.VMEM(grads.shape, jnp.float32),
            pltpu.VMEM(forward_s.shape, jnp.bfloat16),
            pltpu.VMEM(inverse_s.shape, jnp.bfloat16),
            pltpu.VMEM(over_l.shape, jnp.float32),
            pltpu.VMEM(out, jnp.float32),
            pltpu.SemaphoreType.DMA((4 + RADIX,)),
        ],
        compiler_params=pltpu.CompilerParams(vmem_limit_bytes=60 << 20),
        cost_estimate=pl.CostEstimate(
            flops=2_500_000_000, bytes_accessed=10_000_000, transcendentals=0
        ),
        name="input_rows",
    )(core, mine, other, grads, forward_s, inverse_s, forward_l, inverse_l, over_l)


def sum_over_chan(value, chan):
    depth = chan // 2

    def moved(array, shift, swap=False):
        ring = []
        for z in range(depth):
            ring.append((2 * z, 2 * ((z + shift) % depth) + swap))
            ring.append((2 * z + 1, 2 * ((z - shift) % depth) + 1 - swap))
        return lax.ppermute(array, "chan", ring)

    value = value + moved(value, 0, True)
    if depth < 2 or depth & (depth - 1):
        total = value
        for shift in range(1, depth):
            total = total + moved(value, shift)
        return total, jnp.zeros_like(total)
    reach = 1
    while 2 * reach < depth:
        value = value + moved(value, reach)
        reach *= 2
    return value, moved(value, 1, True)


def local(saved_input, out_grad, filters):
    batch, channels, tokens = saved_input.shape
    groups = filters.shape[0]
    devices = lax.axis_size("ctx")
    chan = lax.axis_size("chan")
    core = lax.axis_index("chan") % 2
    part = tokens // (RADIX * LANES)
    consts = tuple(jnp.asarray(t) for t in tables())
    packed = laid_out(core.reshape(1), saved_input, out_grad, filters)
    rows = lax.all_to_all(packed, "ctx", 0, 0, tiled=True)
    terms, grads, mine = filter_terms(rows, consts)
    other = lax.ppermute(mine, "chan", [(i, i ^ 1) for i in range(chan)])
    terms = lax.all_to_all(terms, "ctx", 0, 0, tiled=True)
    inputs = input_rows(core.reshape(1), mine, other, grads, consts)
    total = jnp.sum(terms.reshape(devices // groups, groups, RADIX, part, LANES), axis=0)
    inputs, total = lax.optimization_barrier((inputs, total))
    inputs = lax.all_to_all(inputs, "ctx", 0, 0, tiled=True)
    inputs = (inputs * (1.0 / TOKENS)).transpose(1, 0, 3, 2, 4)
    input_grad = inputs.reshape(batch, channels, tokens).astype(jnp.bfloat16)
    total, last = sum_over_chan(total, chan)
    input_grad, last = lax.optimization_barrier((input_grad, last))
    total = total + last
    per_filter = channels // groups
    norm = float(tokens * devices * batch * per_filter * chan) ** -0.5
    filter_grad = total.swapaxes(1, 2).reshape(groups, tokens) * (norm / TOKENS)
    return input_grad, filter_grad


def solution(mesh):
    placed = (P(None, "chan", "ctx"), P(None, "chan", "ctx"), P(None, "ctx"))
    return jax.shard_map(
        local,
        mesh=mesh,
        in_specs=placed,
        out_specs=(P(None, "chan", "ctx"), P(None, "ctx")),
        check_vma=False,
    )
```

```python
import functools
import math

import jax
import jax.numpy as jnp
import ml_dtypes
import numpy as np
from jax import lax
from jax.experimental import pallas as pl
from jax.experimental.pallas import tpu as pltpu
from jax.sharding import PartitionSpec as P

RADIX = 8
SIDE = 128
TOKENS = RADIX * SIDE * SIDE
LANES = 128
STEP = 32


def two_halves(matrix):
    high = matrix.astype(ml_dtypes.bfloat16)
    low = (matrix - high.astype(np.float64)).astype(ml_dtypes.bfloat16)
    return high, low


@functools.cache
def tables():
    side = np.arange(SIDE)
    turn = np.pi / 2 + 2 * np.pi * side
    forward_s, inverse_s = [], []
    for r in range(RADIX):
        matrix = np.exp(1j * np.outer(turn, side + r / RADIX) / SIDE)
        high, low = two_halves(np.concatenate([matrix.real, matrix.imag], axis=0))
        forward_s.append(np.concatenate([high, low], axis=0))
        high, low = two_halves(np.concatenate([matrix.real.T, matrix.imag.T], axis=1))
        inverse_s.append(np.concatenate([high, low], axis=0))
    over_r = np.exp(1j * np.outer(np.arange(RADIX), turn) / (RADIX * SIDE))
    over_r = np.stack([over_r.real, over_r.imag], axis=1)[..., None]
    over_r = np.broadcast_to(over_r, (RADIX, 2, SIDE, LANES)).astype(np.float32)
    q = np.arange(RADIX)[:, None, None]
    over_l = np.exp(1j * side * (turn[:, None] + 256 * np.pi * q) / TOKENS)
    over_l = np.stack([over_l.real, over_l.imag], axis=1).astype(np.float32)
    matrix = np.exp(2j * np.pi * np.outer(side, side) / SIDE)
    form = np.block([[matrix.real, matrix.imag], [-matrix.imag, matrix.real]])
    forward_l = np.stack(two_halves(form))
    inverse_l = np.stack(two_halves(form.T))
    return np.stack(forward_s), np.stack(inverse_s), forward_l, inverse_l, over_r, over_l


def dft4(a, b, c, d, sign):
    t0 = (a[0] + c[0], a[1] + c[1])
    t1 = (a[0] - c[0], a[1] - c[1])
    t2 = (b[0] + d[0], b[1] + d[1])
    t3 = (b[0] - d[0], b[1] - d[1])
    if sign < 0:
        t3 = (-t3[0], -t3[1])
    return [
        (t0[0] + t2[0], t0[1] + t2[1]),
        (t1[0] - t3[1], t1[1] + t3[0]),
        (t0[0] - t2[0], t0[1] - t2[1]),
        (t1[0] + t3[1], t1[1] - t3[0]),
    ]


def dft8(u, sign):
    even = dft4(u[0], u[2], u[4], u[6], sign)
    odd = dft4(u[1], u[3], u[5], u[7], sign)
    half = math.sqrt(0.5)
    turned = [
        odd[0],
        (half * (odd[1][0] - sign * odd[1][1]), half * (odd[1][1] + sign * odd[1][0])),
        (-sign * odd[2][1], sign * odd[2][0]),
        (half * (-odd[3][0] - sign * odd[3][1]), half * (sign * odd[3][0] - odd[3][1])),
    ]
    plus = [(e[0] + o[0], e[1] + o[1]) for e, o in zip(even, turned)]
    minus = [(e[0] - o[0], e[1] - o[1]) for e, o in zip(even, turned)]
    return plus + minus


def split(values):
    high = values.astype(jnp.bfloat16)
    low = (values - high.astype(jnp.float32)).astype(jnp.bfloat16)
    return high, low


def dot(left, right):
    return jnp.dot(left, right, preferred_element_type=jnp.float32)


def dot_from_right(values, table):
    high, low = split(values)
    count = values.shape[0]
    both = dot(jnp.concatenate([high, low], axis=0), table[0])
    return both[:count] + both[count:] + dot(high, table[1])


def times(a, b):
    return a[0] * b[0] - a[1] * b[1], a[0] * b[1] + a[1] * b[0]


def times_conjugate(a, b):
    return a[0] * b[0] + a[1] * b[1], a[1] * b[0] - a[0] * b[1]


def parts(values):
    return values[:, :LANES], values[:, LANES:]


def over_s_forward(blocks_of, rows, radices, forward_s, z):
    for r in radices:
        samples = [blocks_of(row, r).reshape(SIDE, LANES) for row in rows]
        high, low = split(jnp.concatenate(samples, axis=1))
        first = forward_s[r, : 2 * SIDE]
        second = forward_s[r, 2 * SIDE :]
        table = jnp.concatenate(
            [
                jnp.concatenate([first, first], axis=1),
                jnp.concatenate([second, jnp.zeros_like(second)], axis=1),
            ],
            axis=0,
        )
        both = dot(table, jnp.concatenate([high, low], axis=0))
        out = both[: 2 * SIDE] + both[2 * SIDE :]
        lanes = pl.ds(rows[0] * LANES, len(rows) * LANES)
        z[r, :, :, lanes] = out.reshape(2, SIDE, len(rows) * LANES)


def over_r_forward(z, row, span, over_l):
    lanes = pl.ds(row * LANES, LANES)
    u = [(z[r, 0, span, lanes], z[r, 1, span, lanes]) for r in range(RADIX)]
    out = []
    for q, value in enumerate(dft8(u, 1)):
        value = times(value, (over_l[q, 0, span, :], over_l[q, 1, span, :]))
        out.append(jnp.concatenate(value, axis=1))
    return out


def over_r_inverse(values, span, over_l):
    v = []
    for q in range(RADIX):
        value = parts(values[q * STEP : (q + 1) * STEP])
        v.append(times_conjugate(value, (over_l[q, 0, span, :], over_l[q, 1, span, :])))
    return dft8(v, -1)


def over_s_inverse(high, low, table):
    both = dot(table, high)
    return both[:SIDE] + both[SIDE:] + dot(table[:SIDE], low)


def filter_kernel(
    rows, forward_s, inverse_s, forward_l, inverse_l, over_r, over_l,
    terms, grads, half, z, back, held, inputs, sems,
):
    half[...] = rows[:, 4 * RADIX :]
    def samples(row, r):
        return rows[:, row * RADIX + r]

    def spectra_of(first_row, span):
        blocks = over_r_forward(z, first_row, span, over_l)
        blocks += over_r_forward(z, first_row + 1, span, over_l)
        return dot_from_right(jnp.concatenate(blocks, axis=0), forward_l)

    over_s_forward(samples, range(2), range(RADIX), forward_s, z)
    size = RADIX * STEP
    steps = SIDE // STEP
    each = RADIX // steps
    for step in range(steps):
        over_s_forward(samples, range(2, 4), range(step * each, (step + 1) * each), forward_s, z)
        inputs[step] = spectra_of(0, pl.ds(step * STEP, STEP))
    copies = []
    for step in range(steps):
        span = pl.ds(step * STEP, STEP)
        spectra = spectra_of(2, span)
        held[step] = spectra
        copies.append(pltpu.make_async_copy(held.at[step], grads.at[step], sems.at[step]))
        first = times_conjugate(parts(spectra[:size]), parts(inputs[step, :size]))
        second = times_conjugate(parts(spectra[size:]), parts(inputs[step, size:]))
        product = jnp.concatenate([first[0] + second[0], first[1] + second[1]], axis=1)
        values = dot_from_right(product, inverse_l)
        for r, value in enumerate(over_r_inverse(values, span, over_l)):
            value = times_conjugate(value, (over_r[r, 0, span, :], over_r[r, 1, span, :]))
            lanes = pl.ds(r * LANES, LANES)
            for part in range(2):
                high, low = split(value[part])
                back[0, part, span, lanes] = high
                back[1, part, span, lanes] = low
    for copy in copies:
        copy.start()
    shape = (2 * SIDE, RADIX * LANES)
    out = over_s_inverse(back[0].reshape(shape), back[1].reshape(shape), inverse_s[...])
    for r in range(RADIX):
        value = out[:, r * LANES : (r + 1) * LANES]
        terms[:, r] = value.reshape(terms.shape[0], terms.shape[2], LANES)
    for copy in copies:
        copy.wait()


def input_kernel(
    core, mine, other, grads, forward_s, inverse_s, forward_l, inverse_l, over_l,
    out, z, back, grads_in, forward_in, inverse_in, turns_in, out_held, sems,
):
    load_forward = pltpu.make_async_copy(forward_s, forward_in, sems.at[3 + RADIX])
    load_forward.start()
    load_turns = pltpu.make_async_copy(over_l, turns_in, sems.at[0])
    load_grads = pltpu.make_async_copy(grads, grads_in, sems.at[1])
    load_inverse = pltpu.make_async_copy(inverse_s, inverse_in, sems.at[2])
    for copy in (load_turns, load_grads, load_inverse):
        copy.start()
    size = RADIX * STEP
    near = core[0] == 0
    per_half = mine.shape[1]

    def filter_block(row, r):
        own, far = mine[:, r % per_half], other[:, r % per_half]
        return jnp.where(near, own, far) if r < per_half else jnp.where(near, far, own)

    load_forward.wait()
    over_s_forward(filter_block, range(1), range(RADIX), forward_in, z)
    load_turns.wait()
    load_grads.wait()
    for step in range(SIDE // STEP):
        span = pl.ds(step * STEP, STEP)
        spectrum = dot_from_right(
            jnp.concatenate(over_r_forward(z, 0, span, turns_in), axis=0), forward_l
        )
        products = []
        for row in range(2):
            grad = grads_in[step, row * size : (row + 1) * size]
            products.append(
                jnp.concatenate(times_conjugate(parts(grad), parts(spectrum)), axis=1)
            )
        values = dot_from_right(jnp.concatenate(products, axis=0), inverse_l)
        for row in range(2):
            lanes = pl.ds(row * LANES, LANES)
            one = values[row * size : (row + 1) * size]
            for r, value in enumerate(over_r_inverse(one, span, turns_in)):
                for part in range(2):
                    high, low = split(value[part])
                    back[0, r, part, span, lanes] = high
                    back[1, r, part, span, lanes] = low
    shape = (2 * SIDE, 2 * LANES)
    load_inverse.wait()
    copies = []
    for r in range(RADIX):
        samples = over_s_inverse(back[0, r].reshape(shape), back[1, r].reshape(shape), inverse_in[r])
        for row in range(2):
            value = samples[:, row * LANES : (row + 1) * LANES]
            out_held[:, row, r] = value.reshape(out.shape[0], out.shape[3], LANES)
        copies.append(pltpu.make_async_copy(out_held.at[:, :, r], out.at[:, :, r], sems.at[3 + r]))
        copies[-1].start()
    for copy in copies:
        copy.wait()


def in_vmem(count):
    return [pl.BlockSpec(memory_space=pltpu.VMEM)] * count


def in_hbm(count):
    return [pl.BlockSpec(memory_space=pltpu.HBM)] * count


def layout_kernel(core, saved_input, out_grad, filters, out, samples, filter_in, sems):
    batch, channels, tokens = saved_input.shape
    groups = filters.shape[0]
    per_half = RADIX // 2
    loads = []
    for array, source in enumerate((saved_input, out_grad)):
        for b in range(batch):
            slot = array * batch + b
            loads.append(pltpu.make_async_copy(source.at[b], samples.at[slot], sems.at[slot]))
    load_filter = pltpu.make_async_copy(filters, filter_in, sems.at[2 * batch])
    for copy in [load_filter, *loads]:
        copy.start()
    load_filter.wait()
    for group in range(groups):
        for r in range(per_half):
            for s in range(tokens // (RADIX * LANES)):
                start = pl.multiple_of((s * RADIX + core[0] * per_half + r) * LANES, LANES)
                row = filter_in[pl.ds(group, 1), pl.ds(start, LANES)]
                out[group, 2 * batch * RADIX + r, pl.ds(s, 1), :] = row
    for channel in range(groups, channels):
        out[channel, 2 * batch * RADIX :] = out[channel % groups, 2 * batch * RADIX :]
    for slot, load in enumerate(loads):
        load.wait()
        for first in range(0, channels, 8):
            for r in range(RADIX):
                for s in range(tokens // (RADIX * LANES)):
                    value = samples[slot, pl.ds(first, 8), pl.ds((s * RADIX + r) * LANES, LANES)]
                    out[pl.ds(first, 8), slot * RADIX + r, s, :] = value


def laid_out(core, saved_input, out_grad, filters):
    arrays = (saved_input, out_grad, filters)
    batch, channels, tokens = saved_input.shape
    part = tokens // (RADIX * LANES)
    tiles = 2 * batch * RADIX + RADIX // 2
    return pl.pallas_call(
        layout_kernel,
        out_shape=jax.ShapeDtypeStruct((channels, tiles, part, LANES), jnp.float32),
        in_specs=[pl.BlockSpec(memory_space=pltpu.SMEM), *in_hbm(3)],
        out_specs=in_vmem(1)[0],
        scratch_shapes=[
            pltpu.VMEM((2 * batch, channels, tokens), jnp.float32),
            pltpu.VMEM(filters.shape, jnp.float32),
            pltpu.SemaphoreType.DMA((2 * batch + 1,)),
        ],
        compiler_params=pltpu.CompilerParams(vmem_limit_bytes=40 << 20),
        name="laid_out",
    )(core, *(pltpu.with_memory_space_constraint(v, pltpu.HBM) for v in arrays))


def filter_terms(rows, consts):
    blocks, tiles, part, lanes = rows.shape
    forward_s, inverse_s, forward_l, inverse_l, over_r, over_l = consts
    steps = SIDE // STEP
    grads = (steps, 2 * RADIX * STEP, 2 * LANES)
    return pl.pallas_call(
        filter_kernel,
        out_shape=(
            jax.ShapeDtypeStruct((blocks, RADIX, part, lanes), jnp.float32),
            pltpu.HBM(grads, jnp.float32),
            jax.ShapeDtypeStruct((blocks, tiles - 4 * RADIX, part, lanes), jnp.float32),
        ),
        in_specs=in_vmem(7),
        out_specs=(in_vmem(1)[0], in_hbm(1)[0], in_vmem(1)[0]),
        scratch_shapes=[
            pltpu.VMEM((RADIX, 2, SIDE, 4 * LANES), jnp.float32),
            pltpu.VMEM((2, 2, SIDE, RADIX * LANES), jnp.bfloat16),
            pltpu.VMEM(grads, jnp.float32),
            pltpu.VMEM(grads, jnp.float32),
            pltpu.SemaphoreType.DMA((steps,)),
        ],
        compiler_params=pltpu.CompilerParams(vmem_limit_bytes=20 << 20),
        cost_estimate=pl.CostEstimate(
            flops=4_000_000_000, bytes_accessed=10_000_000, transcendentals=0
        ),
        name="filter_terms",
    )(rows, forward_s, inverse_s[0], forward_l, inverse_l, over_r, over_l)


def input_rows(core, mine, other, grads, consts):
    blocks, tiles, part, lanes = mine.shape
    forward_s, inverse_s, forward_l, inverse_l, _, over_l = consts
    out = (blocks, 2, RADIX, part, lanes)
    return pl.pallas_call(
        input_kernel,
        out_shape=jax.ShapeDtypeStruct(out, jnp.float32),
        in_specs=[
            pl.BlockSpec(memory_space=pltpu.SMEM),
            *in_vmem(2),
            *in_hbm(3),
            *in_vmem(2),
            *in_hbm(1),
        ],
        out_specs=in_hbm(1)[0],
        scratch_shapes=[
            pltpu.VMEM((RADIX, 2, SIDE, LANES), jnp.float32),
            pltpu.VMEM((2, RADIX, 2, SIDE, 2 * LANES), jnp.bfloat16),
            pltpu.VMEM(grads.shape, jnp.float32),
            pltpu.VMEM(forward_s.shape, jnp.bfloat16),
            pltpu.VMEM(inverse_s.shape, jnp.bfloat16),
            pltpu.VMEM(over_l.shape, jnp.float32),
            pltpu.VMEM(out, jnp.float32),
            pltpu.SemaphoreType.DMA((4 + RADIX,)),
        ],
        compiler_params=pltpu.CompilerParams(vmem_limit_bytes=60 << 20),
        cost_estimate=pl.CostEstimate(
            flops=2_500_000_000, bytes_accessed=10_000_000, transcendentals=0
        ),
        name="input_rows",
    )(core, mine, other, grads, forward_s, inverse_s, forward_l, inverse_l, over_l)


def sum_over_chan(value, chan):
    depth = chan // 2

    def moved(array, shift, swap=False):
        ring = []
        for z in range(depth):
            ring.append((2 * z, 2 * ((z + shift) % depth) + swap))
            ring.append((2 * z + 1, 2 * ((z - shift) % depth) + 1 - swap))
        return lax.ppermute(array, "chan", ring)

    value = value + moved(value, 0, True)
    if depth < 2 or depth & (depth - 1):
        total = value
        for shift in range(1, depth):
            total = total + moved(value, shift)
        return total, jnp.zeros_like(total)
    reach = 1
    while 2 * reach < depth:
        value = value + moved(value, reach)
        reach *= 2
    return value, moved(value, 1, True)


def local(saved_input, out_grad, filters):
    batch, channels, tokens = saved_input.shape
    groups = filters.shape[0]
    devices = lax.axis_size("ctx")
    chan = lax.axis_size("chan")
    core = lax.axis_index("chan") % 2
    part = tokens // (RADIX * LANES)
    consts = tuple(jnp.asarray(t) for t in tables())
    packed = laid_out(core.reshape(1), saved_input, out_grad, filters)
    rows = lax.all_to_all(packed, "ctx", 0, 0, tiled=True)
    terms, grads, mine = filter_terms(rows, consts)
    other = lax.ppermute(mine, "chan", [(i, i ^ 1) for i in range(chan)])
    terms = lax.all_to_all(terms, "ctx", 0, 0, tiled=True)
    inputs = input_rows(core.reshape(1), mine, other, grads, consts)
    total = jnp.sum(terms.reshape(devices // groups, groups, RADIX, part, LANES), axis=0)
    inputs, total = lax.optimization_barrier((inputs, total))
    inputs = lax.all_to_all(inputs, "ctx", 0, 0, tiled=True)
    inputs = (inputs * (1.0 / TOKENS)).transpose(1, 0, 3, 2, 4)
    input_grad = inputs.reshape(batch, channels, tokens).astype(jnp.bfloat16)
    total, last = sum_over_chan(total, chan)
    input_grad, last = lax.optimization_barrier((input_grad, last))
    total = total + last
    per_filter = channels // groups
    norm = float(tokens * devices * batch * per_filter * chan) ** -0.5
    filter_grad = total.swapaxes(1, 2).reshape(groups, tokens) * (norm / TOKENS)
    return input_grad, filter_grad


def solution(mesh):
    placed = (P(None, "chan", "ctx"), P(None, "chan", "ctx"), P(None, "ctx"))
    return jax.shard_map(
        local,
        mesh=mesh,
        in_specs=placed,
        out_specs=(P(None, "chan", "ctx"), P(None, "ctx")),
        check_vma=False,
    )
```

```python
import functools
import math

import jax
import jax.numpy as jnp
import ml_dtypes
import numpy as np
from jax import lax
from jax.experimental import pallas as pl
from jax.experimental.pallas import tpu as pltpu
from jax.sharding import PartitionSpec as P

RADIX = 8
SIDE = 128
TOKENS = RADIX * SIDE * SIDE
LANES = 128
STEP = 32


def two_halves(matrix):
    high = matrix.astype(ml_dtypes.bfloat16)
    low = (matrix - high.astype(np.float64)).astype(ml_dtypes.bfloat16)
    return high, low


@functools.cache
def tables():
    side = np.arange(SIDE)
    turn = np.pi / 2 + 2 * np.pi * side
    forward_s, inverse_s = [], []
    for r in range(RADIX):
        matrix = np.exp(1j * np.outer(turn, side + r / RADIX) / SIDE)
        high, low = two_halves(np.concatenate([matrix.real, matrix.imag], axis=0))
        forward_s.append(np.concatenate([high, low], axis=0))
        high, low = two_halves(np.concatenate([matrix.real.T, matrix.imag.T], axis=1))
        inverse_s.append(np.concatenate([high, low], axis=0))
    over_r = np.exp(1j * np.outer(np.arange(RADIX), turn) / (RADIX * SIDE))
    over_r = np.stack([over_r.real, over_r.imag], axis=1)[..., None]
    over_r = np.broadcast_to(over_r, (RADIX, 2, SIDE, LANES)).astype(np.float32)
    q = np.arange(RADIX)[:, None, None]
    over_l = np.exp(1j * side * (turn[:, None] + 256 * np.pi * q) / TOKENS)
    over_l = np.stack([over_l.real, over_l.imag], axis=1).astype(np.float32)
    matrix = np.exp(2j * np.pi * np.outer(side, side) / SIDE)
    form = np.block([[matrix.real, matrix.imag], [-matrix.imag, matrix.real]])
    forward_l = np.stack(two_halves(form))
    inverse_l = np.stack(two_halves(form.T))
    return np.stack(forward_s), np.stack(inverse_s), forward_l, inverse_l, over_r, over_l


def dft4(a, b, c, d, sign):
    t0 = (a[0] + c[0], a[1] + c[1])
    t1 = (a[0] - c[0], a[1] - c[1])
    t2 = (b[0] + d[0], b[1] + d[1])
    t3 = (b[0] - d[0], b[1] - d[1])
    if sign < 0:
        t3 = (-t3[0], -t3[1])
    return [
        (t0[0] + t2[0], t0[1] + t2[1]),
        (t1[0] - t3[1], t1[1] + t3[0]),
        (t0[0] - t2[0], t0[1] - t2[1]),
        (t1[0] + t3[1], t1[1] - t3[0]),
    ]


def dft8(u, sign):
    even = dft4(u[0], u[2], u[4], u[6], sign)
    odd = dft4(u[1], u[3], u[5], u[7], sign)
    half = math.sqrt(0.5)
    turned = [
        odd[0],
        (half * (odd[1][0] - sign * odd[1][1]), half * (odd[1][1] + sign * odd[1][0])),
        (-sign * odd[2][1], sign * odd[2][0]),
        (half * (-odd[3][0] - sign * odd[3][1]), half * (sign * odd[3][0] - odd[3][1])),
    ]
    plus = [(e[0] + o[0], e[1] + o[1]) for e, o in zip(even, turned)]
    minus = [(e[0] - o[0], e[1] - o[1]) for e, o in zip(even, turned)]
    return plus + minus


def split(values):
    high = values.astype(jnp.bfloat16)
    low = (values - high.astype(jnp.float32)).astype(jnp.bfloat16)
    return high, low


def dot(left, right):
    return jnp.dot(left, right, preferred_element_type=jnp.float32)


def dot_from_right(values, table):
    high, low = split(values)
    count = values.shape[0]
    both = dot(jnp.concatenate([high, low], axis=0), table[0])
    return both[:count] + both[count:] + dot(high, table[1])


def times(a, b):
    return a[0] * b[0] - a[1] * b[1], a[0] * b[1] + a[1] * b[0]


def times_conjugate(a, b):
    return a[0] * b[0] + a[1] * b[1], a[1] * b[0] - a[0] * b[1]


def parts(values):
    return values[:, :LANES], values[:, LANES:]


def over_s_forward(blocks_of, rows, radices, forward_s, z):
    for r in radices:
        samples = [blocks_of(row, r).reshape(SIDE, LANES) for row in rows]
        high, low = split(jnp.concatenate(samples, axis=1))
        first = forward_s[r, : 2 * SIDE]
        second = forward_s[r, 2 * SIDE :]
        table = jnp.concatenate(
            [
                jnp.concatenate([first, first], axis=1),
                jnp.concatenate([second, jnp.zeros_like(second)], axis=1),
            ],
            axis=0,
        )
        both = dot(table, jnp.concatenate([high, low], axis=0))
        out = both[: 2 * SIDE] + both[2 * SIDE :]
        lanes = pl.ds(rows[0] * LANES, len(rows) * LANES)
        z[r, :, :, lanes] = out.reshape(2, SIDE, len(rows) * LANES)


def over_r_forward(z, row, span, over_l):
    lanes = pl.ds(row * LANES, LANES)
    u = [(z[r, 0, span, lanes], z[r, 1, span, lanes]) for r in range(RADIX)]
    out = []
    for q, value in enumerate(dft8(u, 1)):
        value = times(value, (over_l[q, 0, span, :], over_l[q, 1, span, :]))
        out.append(jnp.concatenate(value, axis=1))
    return out


def over_r_inverse(values, span, over_l):
    v = []
    for q in range(RADIX):
        value = parts(values[q * STEP : (q + 1) * STEP])
        v.append(times_conjugate(value, (over_l[q, 0, span, :], over_l[q, 1, span, :])))
    return dft8(v, -1)


def over_s_inverse(high, low, table):
    both = dot(table, high)
    return both[:SIDE] + both[SIDE:] + dot(table[:SIDE], low)


def filter_kernel(
    rows, forward_s, inverse_s, forward_l, inverse_l, over_r, over_l,
    terms, grads, half, z, back, held, inputs, sems,
):
    half[...] = rows[:, 4 * RADIX :]
    def samples(row, r):
        return rows[:, row * RADIX + r]

    def spectra_of(first_row, span):
        blocks = over_r_forward(z, first_row, span, over_l)
        blocks += over_r_forward(z, first_row + 1, span, over_l)
        return dot_from_right(jnp.concatenate(blocks, axis=0), forward_l)

    over_s_forward(samples, range(2), range(RADIX), forward_s, z)
    size = RADIX * STEP
    steps = SIDE // STEP
    each = RADIX // steps
    for step in range(steps):
        over_s_forward(samples, range(2, 4), range(step * each, (step + 1) * each), forward_s, z)
        inputs[step] = spectra_of(0, pl.ds(step * STEP, STEP))
    copies = []
    following = spectra_of(2, pl.ds(0, STEP))
    for step in range(steps):
        span = pl.ds(step * STEP, STEP)
        spectra = following
        if step + 1 < steps:
            following = spectra_of(2, pl.ds((step + 1) * STEP, STEP))
        held[step] = spectra
        copies.append(pltpu.make_async_copy(held.at[step], grads.at[step], sems.at[step]))
        first = times_conjugate(parts(spectra[:size]), parts(inputs[step, :size]))
        second = times_conjugate(parts(spectra[size:]), parts(inputs[step, size:]))
        product = jnp.concatenate([first[0] + second[0], first[1] + second[1]], axis=1)
        values = dot_from_right(product, inverse_l)
        for r, value in enumerate(over_r_inverse(values, span, over_l)):
            value = times_conjugate(value, (over_r[r, 0, span, :], over_r[r, 1, span, :]))
            lanes = pl.ds(r * LANES, LANES)
            for part in range(2):
                high, low = split(value[part])
                back[0, part, span, lanes] = high
                back[1, part, span, lanes] = low
    for copy in copies:
        copy.start()
    shape = (2 * SIDE, RADIX * LANES)
    out = over_s_inverse(back[0].reshape(shape), back[1].reshape(shape), inverse_s[...])
    for r in range(RADIX):
        value = out[:, r * LANES : (r + 1) * LANES]
        terms[:, r] = value.reshape(terms.shape[0], terms.shape[2], LANES)
    for copy in copies:
        copy.wait()


def input_kernel(
    core, mine, other, grads, forward_s, inverse_s, forward_l, inverse_l, over_l,
    out, z, back, grads_in, forward_in, inverse_in, turns_in, out_held, sems,
):
    load_forward = pltpu.make_async_copy(forward_s, forward_in, sems.at[3 + RADIX])
    load_forward.start()
    load_turns = pltpu.make_async_copy(over_l, turns_in, sems.at[0])
    load_grads = pltpu.make_async_copy(grads, grads_in, sems.at[1])
    load_inverse = pltpu.make_async_copy(inverse_s, inverse_in, sems.at[2])
    for copy in (load_turns, load_grads, load_inverse):
        copy.start()
    size = RADIX * STEP
    near = core[0] == 0
    per_half = mine.shape[1]

    def filter_block(row, r):
        own, far = mine[:, r % per_half], other[:, r % per_half]
        return jnp.where(near, own, far) if r < per_half else jnp.where(near, far, own)

    load_forward.wait()
    over_s_forward(filter_block, range(1), range(RADIX), forward_in, z)
    load_turns.wait()
    load_grads.wait()
    for step in range(SIDE // STEP):
        span = pl.ds(step * STEP, STEP)
        spectrum = dot_from_right(
            jnp.concatenate(over_r_forward(z, 0, span, turns_in), axis=0), forward_l
        )
        products = []
        for row in range(2):
            grad = grads_in[step, row * size : (row + 1) * size]
            products.append(
                jnp.concatenate(times_conjugate(parts(grad), parts(spectrum)), axis=1)
            )
        values = dot_from_right(jnp.concatenate(products, axis=0), inverse_l)
        for row in range(2):
            lanes = pl.ds(row * LANES, LANES)
            one = values[row * size : (row + 1) * size]
            for r, value in enumerate(over_r_inverse(one, span, turns_in)):
                for part in range(2):
                    high, low = split(value[part])
                    back[0, r, part, span, lanes] = high
                    back[1, r, part, span, lanes] = low
    shape = (2 * SIDE, 2 * LANES)
    load_inverse.wait()
    copies = []
    for r in range(RADIX):
        samples = over_s_inverse(back[0, r].reshape(shape), back[1, r].reshape(shape), inverse_in[r])
        for row in range(2):
            value = samples[:, row * LANES : (row + 1) * LANES]
            out_held[:, row, r] = value.reshape(out.shape[0], out.shape[3], LANES)
        copies.append(pltpu.make_async_copy(out_held.at[:, :, r], out.at[:, :, r], sems.at[3 + r]))
        copies[-1].start()
    for copy in copies:
        copy.wait()


def in_vmem(count):
    return [pl.BlockSpec(memory_space=pltpu.VMEM)] * count


def in_hbm(count):
    return [pl.BlockSpec(memory_space=pltpu.HBM)] * count


def layout_kernel(core, saved_input, out_grad, filters, out, samples, filter_in, sems):
    batch, channels, tokens = saved_input.shape
    groups = filters.shape[0]
    per_half = RADIX // 2
    loads = []
    for array, source in enumerate((saved_input, out_grad)):
        for b in range(batch):
            slot = array * batch + b
            loads.append(pltpu.make_async_copy(source.at[b], samples.at[slot], sems.at[slot]))
    load_filter = pltpu.make_async_copy(filters, filter_in, sems.at[2 * batch])
    for copy in [load_filter, *loads]:
        copy.start()
    load_filter.wait()
    for group in range(groups):
        for r in range(per_half):
            for s in range(tokens // (RADIX * LANES)):
                start = pl.multiple_of((s * RADIX + core[0] * per_half + r) * LANES, LANES)
                row = filter_in[pl.ds(group, 1), pl.ds(start, LANES)]
                out[group, 2 * batch * RADIX + r, pl.ds(s, 1), :] = row
    for channel in range(groups, channels):
        out[channel, 2 * batch * RADIX :] = out[channel % groups, 2 * batch * RADIX :]
    for slot, load in enumerate(loads):
        load.wait()
        for first in range(0, channels, 8):
            for r in range(RADIX):
                for s in range(tokens // (RADIX * LANES)):
                    value = samples[slot, pl.ds(first, 8), pl.ds((s * RADIX + r) * LANES, LANES)]
                    out[pl.ds(first, 8), slot * RADIX + r, s, :] = value


def laid_out(core, saved_input, out_grad, filters):
    arrays = (saved_input, out_grad, filters)
    batch, channels, tokens = saved_input.shape
    part = tokens // (RADIX * LANES)
    tiles = 2 * batch * RADIX + RADIX // 2
    return pl.pallas_call(
        layout_kernel,
        out_shape=jax.ShapeDtypeStruct((channels, tiles, part, LANES), jnp.float32),
        in_specs=[pl.BlockSpec(memory_space=pltpu.SMEM), *in_hbm(3)],
        out_specs=in_vmem(1)[0],
        scratch_shapes=[
            pltpu.VMEM((2 * batch, channels, tokens), jnp.float32),
            pltpu.VMEM(filters.shape, jnp.float32),
            pltpu.SemaphoreType.DMA((2 * batch + 1,)),
        ],
        compiler_params=pltpu.CompilerParams(vmem_limit_bytes=40 << 20),
        name="laid_out",
    )(core, *(pltpu.with_memory_space_constraint(v, pltpu.HBM) for v in arrays))


def filter_terms(rows, consts):
    blocks, tiles, part, lanes = rows.shape
    forward_s, inverse_s, forward_l, inverse_l, over_r, over_l = consts
    steps = SIDE // STEP
    grads = (steps, 2 * RADIX * STEP, 2 * LANES)
    return pl.pallas_call(
        filter_kernel,
        out_shape=(
            jax.ShapeDtypeStruct((blocks, RADIX, part, lanes), jnp.float32),
            pltpu.HBM(grads, jnp.float32),
            jax.ShapeDtypeStruct((blocks, tiles - 4 * RADIX, part, lanes), jnp.float32),
        ),
        in_specs=in_vmem(7),
        out_specs=(in_vmem(1)[0], in_hbm(1)[0], in_vmem(1)[0]),
        scratch_shapes=[
            pltpu.VMEM((RADIX, 2, SIDE, 4 * LANES), jnp.float32),
            pltpu.VMEM((2, 2, SIDE, RADIX * LANES), jnp.bfloat16),
            pltpu.VMEM(grads, jnp.float32),
            pltpu.VMEM(grads, jnp.float32),
            pltpu.SemaphoreType.DMA((steps,)),
        ],
        compiler_params=pltpu.CompilerParams(vmem_limit_bytes=20 << 20),
        cost_estimate=pl.CostEstimate(
            flops=4_000_000_000, bytes_accessed=10_000_000, transcendentals=0
        ),
        name="filter_terms",
    )(rows, forward_s, inverse_s[0], forward_l, inverse_l, over_r, over_l)


def input_rows(core, mine, other, grads, consts):
    blocks, tiles, part, lanes = mine.shape
    forward_s, inverse_s, forward_l, inverse_l, _, over_l = consts
    out = (blocks, 2, RADIX, part, lanes)
    return pl.pallas_call(
        input_kernel,
        out_shape=jax.ShapeDtypeStruct(out, jnp.float32),
        in_specs=[
            pl.BlockSpec(memory_space=pltpu.SMEM),
            *in_vmem(2),
            *in_hbm(3),
            *in_vmem(2),
            *in_hbm(1),
        ],
        out_specs=in_hbm(1)[0],
        scratch_shapes=[
            pltpu.VMEM((RADIX, 2, SIDE, LANES), jnp.float32),
            pltpu.VMEM((2, RADIX, 2, SIDE, 2 * LANES), jnp.bfloat16),
            pltpu.VMEM(grads.shape, jnp.float32),
            pltpu.VMEM(forward_s.shape, jnp.bfloat16),
            pltpu.VMEM(inverse_s.shape, jnp.bfloat16),
            pltpu.VMEM(over_l.shape, jnp.float32),
            pltpu.VMEM(out, jnp.float32),
            pltpu.SemaphoreType.DMA((4 + RADIX,)),
        ],
        compiler_params=pltpu.CompilerParams(vmem_limit_bytes=60 << 20),
        cost_estimate=pl.CostEstimate(
            flops=2_500_000_000, bytes_accessed=10_000_000, transcendentals=0
        ),
        name="input_rows",
    )(core, mine, other, grads, forward_s, inverse_s, forward_l, inverse_l, over_l)


def sum_over_chan(value, chan):
    depth = chan // 2

    def moved(array, shift, swap=False):
        ring = []
        for z in range(depth):
            ring.append((2 * z, 2 * ((z + shift) % depth) + swap))
            ring.append((2 * z + 1, 2 * ((z - shift) % depth) + 1 - swap))
        return lax.ppermute(array, "chan", ring)

    value = value + moved(value, 0, True)
    if depth < 2 or depth & (depth - 1):
        total = value
        for shift in range(1, depth):
            total = total + moved(value, shift)
        return total, jnp.zeros_like(total)
    reach = 1
    while 2 * reach < depth:
        value = value + moved(value, reach)
        reach *= 2
    return value, moved(value, 1, True)


def local(saved_input, out_grad, filters):
    batch, channels, tokens = saved_input.shape
    groups = filters.shape[0]
    devices = lax.axis_size("ctx")
    chan = lax.axis_size("chan")
    core = lax.axis_index("chan") % 2
    part = tokens // (RADIX * LANES)
    consts = tuple(jnp.asarray(t) for t in tables())
    packed = laid_out(core.reshape(1), saved_input, out_grad, filters)
    rows = lax.all_to_all(packed, "ctx", 0, 0, tiled=True)
    terms, grads, mine = filter_terms(rows, consts)
    other = lax.ppermute(mine, "chan", [(i, i ^ 1) for i in range(chan)])
    terms = lax.all_to_all(terms, "ctx", 0, 0, tiled=True)
    inputs = input_rows(core.reshape(1), mine, other, grads, consts)
    total = jnp.sum(terms.reshape(devices // groups, groups, RADIX, part, LANES), axis=0)
    inputs, total = lax.optimization_barrier((inputs, total))
    inputs = lax.all_to_all(inputs, "ctx", 0, 0, tiled=True)
    inputs = (inputs * (1.0 / TOKENS)).transpose(1, 0, 3, 2, 4)
    input_grad = inputs.reshape(batch, channels, tokens).astype(jnp.bfloat16)
    total, last = sum_over_chan(total, chan)
    input_grad, last = lax.optimization_barrier((input_grad, last))
    total = total + last
    per_filter = channels // groups
    norm = float(tokens * devices * batch * per_filter * chan) ** -0.5
    filter_grad = total.swapaxes(1, 2).reshape(groups, tokens) * (norm / TOKENS)
    return input_grad, filter_grad


def solution(mesh):
    placed = (P(None, "chan", "ctx"), P(None, "chan", "ctx"), P(None, "ctx"))
    return jax.shard_map(
        local,
        mesh=mesh,
        in_specs=placed,
        out_specs=(P(None, "chan", "ctx"), P(None, "ctx")),
        check_vma=False,
    )
```

```python
import functools
import math

import jax
import jax.numpy as jnp
import ml_dtypes
import numpy as np
from jax import lax
from jax.experimental import pallas as pl
from jax.experimental.pallas import tpu as pltpu
from jax.sharding import PartitionSpec as P

RADIX = 8
SIDE = 128
TOKENS = RADIX * SIDE * SIDE
LANES = 128
STEP = 32


def two_halves(matrix):
    high = matrix.astype(ml_dtypes.bfloat16)
    low = (matrix - high.astype(np.float64)).astype(ml_dtypes.bfloat16)
    return high, low


@functools.cache
def tables():
    side = np.arange(SIDE)
    turn = np.pi / 2 + 2 * np.pi * side
    forward_s, inverse_s = [], []
    for r in range(RADIX):
        matrix = np.exp(1j * np.outer(turn, side + r / RADIX) / SIDE)
        high, low = two_halves(np.concatenate([matrix.real, matrix.imag], axis=0))
        forward_s.append(np.concatenate([high, low], axis=0))
        high, low = two_halves(np.concatenate([matrix.real.T, matrix.imag.T], axis=1))
        inverse_s.append(np.concatenate([high, low], axis=0))
    over_r = np.exp(1j * np.outer(np.arange(RADIX), turn) / (RADIX * SIDE))
    over_r = np.stack([over_r.real, over_r.imag], axis=1)[..., None]
    over_r = np.broadcast_to(over_r, (RADIX, 2, SIDE, LANES)).astype(np.float32)
    q = np.arange(RADIX)[:, None, None]
    over_l = np.exp(1j * side * (turn[:, None] + 256 * np.pi * q) / TOKENS)
    over_l = np.stack([over_l.real, over_l.imag], axis=1).astype(np.float32)
    matrix = np.exp(2j * np.pi * np.outer(side, side) / SIDE)
    form = np.block([[matrix.real, matrix.imag], [-matrix.imag, matrix.real]])
    forward_l = np.stack(two_halves(form))
    inverse_l = np.stack(two_halves(form.T))
    return np.stack(forward_s), np.stack(inverse_s), forward_l, inverse_l, over_r, over_l


def dft4(a, b, c, d, sign):
    t0 = (a[0] + c[0], a[1] + c[1])
    t1 = (a[0] - c[0], a[1] - c[1])
    t2 = (b[0] + d[0], b[1] + d[1])
    t3 = (b[0] - d[0], b[1] - d[1])
    if sign < 0:
        t3 = (-t3[0], -t3[1])
    return [
        (t0[0] + t2[0], t0[1] + t2[1]),
        (t1[0] - t3[1], t1[1] + t3[0]),
        (t0[0] - t2[0], t0[1] - t2[1]),
        (t1[0] + t3[1], t1[1] - t3[0]),
    ]


def dft8(u, sign):
    even = dft4(u[0], u[2], u[4], u[6], sign)
    odd = dft4(u[1], u[3], u[5], u[7], sign)
    half = math.sqrt(0.5)
    turned = [
        odd[0],
        (half * (odd[1][0] - sign * odd[1][1]), half * (odd[1][1] + sign * odd[1][0])),
        (-sign * odd[2][1], sign * odd[2][0]),
        (half * (-odd[3][0] - sign * odd[3][1]), half * (sign * odd[3][0] - odd[3][1])),
    ]
    plus = [(e[0] + o[0], e[1] + o[1]) for e, o in zip(even, turned)]
    minus = [(e[0] - o[0], e[1] - o[1]) for e, o in zip(even, turned)]
    return plus + minus


def split(values):
    high = values.astype(jnp.bfloat16)
    low = (values - high.astype(jnp.float32)).astype(jnp.bfloat16)
    return high, low


def dot(left, right):
    return jnp.dot(left, right, preferred_element_type=jnp.float32)


def dot_from_right(values, table):
    high, low = split(values)
    count = values.shape[0]
    both = dot(jnp.concatenate([high, low], axis=0), table[0])
    return both[:count] + both[count:] + dot(high, table[1])


def times(a, b):
    return a[0] * b[0] - a[1] * b[1], a[0] * b[1] + a[1] * b[0]


def times_conjugate(a, b):
    return a[0] * b[0] + a[1] * b[1], a[1] * b[0] - a[0] * b[1]


def parts(values):
    return values[:, :LANES], values[:, LANES:]


def over_s_forward(blocks_of, rows, radices, forward_s, z):
    for r in radices:
        samples = [blocks_of(row, r).reshape(SIDE, LANES) for row in rows]
        high, low = split(jnp.concatenate(samples, axis=1))
        first = forward_s[r, : 2 * SIDE]
        second = forward_s[r, 2 * SIDE :]
        table = jnp.concatenate(
            [
                jnp.concatenate([first, first], axis=1),
                jnp.concatenate([second, jnp.zeros_like(second)], axis=1),
            ],
            axis=0,
        )
        both = dot(table, jnp.concatenate([high, low], axis=0))
        out = both[: 2 * SIDE] + both[2 * SIDE :]
        lanes = pl.ds(rows[0] * LANES, len(rows) * LANES)
        z[r, :, :, lanes] = out.reshape(2, SIDE, len(rows) * LANES)


def over_r_forward(z, row, span, over_l):
    lanes = pl.ds(row * LANES, LANES)
    u = [(z[r, 0, span, lanes], z[r, 1, span, lanes]) for r in range(RADIX)]
    out = []
    for q, value in enumerate(dft8(u, 1)):
        value = times(value, (over_l[q, 0, span, :], over_l[q, 1, span, :]))
        out.append(jnp.concatenate(value, axis=1))
    return out


def over_r_inverse(values, span, over_l):
    v = []
    for q in range(RADIX):
        value = parts(values[q * STEP : (q + 1) * STEP])
        v.append(times_conjugate(value, (over_l[q, 0, span, :], over_l[q, 1, span, :])))
    return dft8(v, -1)


def over_s_inverse(high, low, table):
    both = dot(table, high)
    return both[:SIDE] + both[SIDE:] + dot(table[:SIDE], low)


def filter_kernel(
    rows, forward_s, inverse_s, forward_l, inverse_l, over_r, over_l,
    terms, grads, half, z, back, held, inputs, sems,
):
    half[...] = rows[:, 4 * RADIX :]
    def samples(row, r):
        return rows[:, row * RADIX + r]

    def spectra_of(first_row, span):
        blocks = over_r_forward(z, first_row, span, over_l)
        blocks += over_r_forward(z, first_row + 1, span, over_l)
        return dot_from_right(jnp.concatenate(blocks, axis=0), forward_l)

    over_s_forward(samples, range(2), range(RADIX), forward_s, z)
    size = RADIX * STEP
    steps = SIDE // STEP
    each = RADIX // steps
    for step in range(steps):
        over_s_forward(samples, range(2, 4), range(step * each, (step + 1) * each), forward_s, z)
        inputs[step] = spectra_of(0, pl.ds(step * STEP, STEP))
    copies = []
    following = spectra_of(2, pl.ds(0, STEP))
    for step in range(steps):
        span = pl.ds(step * STEP, STEP)
        spectra = following
        if step + 1 < steps:
            following = spectra_of(2, pl.ds((step + 1) * STEP, STEP))
        held[step] = spectra
        copies.append(pltpu.make_async_copy(held.at[step], grads.at[step], sems.at[step]))
        first = times_conjugate(parts(spectra[:size]), parts(inputs[step, :size]))
        second = times_conjugate(parts(spectra[size:]), parts(inputs[step, size:]))
        product = jnp.concatenate([first[0] + second[0], first[1] + second[1]], axis=1)
        values = dot_from_right(product, inverse_l)
        for r, value in enumerate(over_r_inverse(values, span, over_l)):
            value = times_conjugate(value, (over_r[r, 0, span, :], over_r[r, 1, span, :]))
            lanes = pl.ds(r * LANES, LANES)
            for part in range(2):
                high, low = split(value[part])
                back[0, part, span, lanes] = high
                back[1, part, span, lanes] = low
    for copy in copies:
        copy.start()
    shape = (2 * SIDE, 2 * LANES)
    for first in range(0, RADIX, 2):
        lanes = pl.ds(first * LANES, 2 * LANES)
        high, low = (back[half_of, :, :, lanes].reshape(shape) for half_of in range(2))
        out = over_s_inverse(high, low, inverse_s[...])
        for r in range(2):
            value = out[:, r * LANES : (r + 1) * LANES]
            terms[:, first + r] = value.reshape(terms.shape[0], terms.shape[2], LANES)
    for copy in copies:
        copy.wait()


def input_kernel(
    core, mine, other, grads, forward_s, inverse_s, forward_l, inverse_l, over_l,
    out, z, back, grads_in, forward_in, inverse_in, turns_in, out_held, sems,
):
    load_forward = pltpu.make_async_copy(forward_s, forward_in, sems.at[3 + RADIX])
    load_forward.start()
    load_turns = pltpu.make_async_copy(over_l, turns_in, sems.at[0])
    load_grads = pltpu.make_async_copy(grads, grads_in, sems.at[1])
    load_inverse = pltpu.make_async_copy(inverse_s, inverse_in, sems.at[2])
    for copy in (load_turns, load_grads, load_inverse):
        copy.start()
    size = RADIX * STEP
    near = core[0] == 0
    per_half = mine.shape[1]

    def filter_block(row, r):
        own, far = mine[:, r % per_half], other[:, r % per_half]
        return jnp.where(near, own, far) if r < per_half else jnp.where(near, far, own)

    load_forward.wait()
    over_s_forward(filter_block, range(1), range(RADIX), forward_in, z)
    load_turns.wait()
    load_grads.wait()
    for step in range(SIDE // STEP):
        span = pl.ds(step * STEP, STEP)
        spectrum = dot_from_right(
            jnp.concatenate(over_r_forward(z, 0, span, turns_in), axis=0), forward_l
        )
        products = []
        for row in range(2):
            grad = grads_in[step, row * size : (row + 1) * size]
            products.append(
                jnp.concatenate(times_conjugate(parts(grad), parts(spectrum)), axis=1)
            )
        values = dot_from_right(jnp.concatenate(products, axis=0), inverse_l)
        for row in range(2):
            lanes = pl.ds(row * LANES, LANES)
            one = values[row * size : (row + 1) * size]
            for r, value in enumerate(over_r_inverse(one, span, turns_in)):
                for part in range(2):
                    high, low = split(value[part])
                    back[0, r, part, span, lanes] = high
                    back[1, r, part, span, lanes] = low
    shape = (2 * SIDE, 2 * LANES)
    load_inverse.wait()
    copies = []
    for r in range(RADIX):
        samples = over_s_inverse(back[0, r].reshape(shape), back[1, r].reshape(shape), inverse_in[r])
        for row in range(2):
            value = samples[:, row * LANES : (row + 1) * LANES]
            out_held[:, row, r] = value.reshape(out.shape[0], out.shape[3], LANES)
        copies.append(pltpu.make_async_copy(out_held.at[:, :, r], out.at[:, :, r], sems.at[3 + r]))
        copies[-1].start()
    for copy in copies:
        copy.wait()


def in_vmem(count):
    return [pl.BlockSpec(memory_space=pltpu.VMEM)] * count


def in_hbm(count):
    return [pl.BlockSpec(memory_space=pltpu.HBM)] * count


def layout_kernel(core, saved_input, out_grad, filters, out, samples, filter_in, sems):
    batch, channels, tokens = saved_input.shape
    groups = filters.shape[0]
    per_half = RADIX // 2
    loads = []
    for array, source in enumerate((saved_input, out_grad)):
        for b in range(batch):
            slot = array * batch + b
            loads.append(pltpu.make_async_copy(source.at[b], samples.at[slot], sems.at[slot]))
    load_filter = pltpu.make_async_copy(filters, filter_in, sems.at[2 * batch])
    for copy in [load_filter, *loads]:
        copy.start()
    load_filter.wait()
    for group in range(groups):
        for r in range(per_half):
            for s in range(tokens // (RADIX * LANES)):
                start = pl.multiple_of((s * RADIX + core[0] * per_half + r) * LANES, LANES)
                row = filter_in[pl.ds(group, 1), pl.ds(start, LANES)]
                out[group, 2 * batch * RADIX + r, pl.ds(s, 1), :] = row
    for channel in range(groups, channels):
        out[channel, 2 * batch * RADIX :] = out[channel % groups, 2 * batch * RADIX :]
    for slot, load in enumerate(loads):
        load.wait()
        for first in range(0, channels, 8):
            for r in range(RADIX):
                for s in range(tokens // (RADIX * LANES)):
                    value = samples[slot, pl.ds(first, 8), pl.ds((s * RADIX + r) * LANES, LANES)]
                    out[pl.ds(first, 8), slot * RADIX + r, s, :] = value


def laid_out(core, saved_input, out_grad, filters):
    arrays = (saved_input, out_grad, filters)
    batch, channels, tokens = saved_input.shape
    part = tokens // (RADIX * LANES)
    tiles = 2 * batch * RADIX + RADIX // 2
    return pl.pallas_call(
        layout_kernel,
        out_shape=jax.ShapeDtypeStruct((channels, tiles, part, LANES), jnp.float32),
        in_specs=[pl.BlockSpec(memory_space=pltpu.SMEM), *in_hbm(3)],
        out_specs=in_vmem(1)[0],
        scratch_shapes=[
            pltpu.VMEM((2 * batch, channels, tokens), jnp.float32),
            pltpu.VMEM(filters.shape, jnp.float32),
            pltpu.SemaphoreType.DMA((2 * batch + 1,)),
        ],
        compiler_params=pltpu.CompilerParams(vmem_limit_bytes=40 << 20),
        name="laid_out",
    )(core, *(pltpu.with_memory_space_constraint(v, pltpu.HBM) for v in arrays))


def filter_terms(rows, consts):
    blocks, tiles, part, lanes = rows.shape
    forward_s, inverse_s, forward_l, inverse_l, over_r, over_l = consts
    steps = SIDE // STEP
    grads = (steps, 2 * RADIX * STEP, 2 * LANES)
    return pl.pallas_call(
        filter_kernel,
        out_shape=(
            jax.ShapeDtypeStruct((blocks, RADIX, part, lanes), jnp.float32),
            pltpu.HBM(grads, jnp.float32),
            jax.ShapeDtypeStruct((blocks, tiles - 4 * RADIX, part, lanes), jnp.float32),
        ),
        in_specs=in_vmem(7),
        out_specs=(in_vmem(1)[0], in_hbm(1)[0], in_vmem(1)[0]),
        scratch_shapes=[
            pltpu.VMEM((RADIX, 2, SIDE, 4 * LANES), jnp.float32),
            pltpu.VMEM((2, 2, SIDE, RADIX * LANES), jnp.bfloat16),
            pltpu.VMEM(grads, jnp.float32),
            pltpu.VMEM(grads, jnp.float32),
            pltpu.SemaphoreType.DMA((steps,)),
        ],
        compiler_params=pltpu.CompilerParams(vmem_limit_bytes=20 << 20),
        cost_estimate=pl.CostEstimate(
            flops=4_000_000_000, bytes_accessed=10_000_000, transcendentals=0
        ),
        name="filter_terms",
    )(rows, forward_s, inverse_s[0], forward_l, inverse_l, over_r, over_l)


def input_rows(core, mine, other, grads, consts):
    blocks, tiles, part, lanes = mine.shape
    forward_s, inverse_s, forward_l, inverse_l, _, over_l = consts
    out = (blocks, 2, RADIX, part, lanes)
    return pl.pallas_call(
        input_kernel,
        out_shape=jax.ShapeDtypeStruct(out, jnp.float32),
        in_specs=[
            pl.BlockSpec(memory_space=pltpu.SMEM),
            *in_vmem(2),
            *in_hbm(3),
            *in_vmem(2),
            *in_hbm(1),
        ],
        out_specs=in_hbm(1)[0],
        scratch_shapes=[
            pltpu.VMEM((RADIX, 2, SIDE, LANES), jnp.float32),
            pltpu.VMEM((2, RADIX, 2, SIDE, 2 * LANES), jnp.bfloat16),
            pltpu.VMEM(grads.shape, jnp.float32),
            pltpu.VMEM(forward_s.shape, jnp.bfloat16),
            pltpu.VMEM(inverse_s.shape, jnp.bfloat16),
            pltpu.VMEM(over_l.shape, jnp.float32),
            pltpu.VMEM(out, jnp.float32),
            pltpu.SemaphoreType.DMA((4 + RADIX,)),
        ],
        compiler_params=pltpu.CompilerParams(vmem_limit_bytes=60 << 20),
        cost_estimate=pl.CostEstimate(
            flops=2_500_000_000, bytes_accessed=10_000_000, transcendentals=0
        ),
        name="input_rows",
    )(core, mine, other, grads, forward_s, inverse_s, forward_l, inverse_l, over_l)


def sum_over_chan(value, chan):
    depth = chan // 2

    def moved(array, shift, swap=False):
        ring = []
        for z in range(depth):
            ring.append((2 * z, 2 * ((z + shift) % depth) + swap))
            ring.append((2 * z + 1, 2 * ((z - shift) % depth) + 1 - swap))
        return lax.ppermute(array, "chan", ring)

    value = value + moved(value, 0, True)
    if depth < 2 or depth & (depth - 1):
        total = value
        for shift in range(1, depth):
            total = total + moved(value, shift)
        return total, jnp.zeros_like(total)
    reach = 1
    while 2 * reach < depth:
        value = value + moved(value, reach)
        reach *= 2
    return value, moved(value, 1, True)


def local(saved_input, out_grad, filters):
    batch, channels, tokens = saved_input.shape
    groups = filters.shape[0]
    devices = lax.axis_size("ctx")
    chan = lax.axis_size("chan")
    core = lax.axis_index("chan") % 2
    part = tokens // (RADIX * LANES)
    consts = tuple(jnp.asarray(t) for t in tables())
    packed = laid_out(core.reshape(1), saved_input, out_grad, filters)
    rows = lax.all_to_all(packed, "ctx", 0, 0, tiled=True)
    terms, grads, mine = filter_terms(rows, consts)
    other = lax.ppermute(mine, "chan", [(i, i ^ 1) for i in range(chan)])
    terms = lax.all_to_all(terms, "ctx", 0, 0, tiled=True)
    inputs = input_rows(core.reshape(1), mine, other, grads, consts)
    total = jnp.sum(terms.reshape(devices // groups, groups, RADIX, part, LANES), axis=0)
    inputs, total = lax.optimization_barrier((inputs, total))
    inputs = lax.all_to_all(inputs, "ctx", 0, 0, tiled=True)
    inputs = (inputs * (1.0 / TOKENS)).transpose(1, 0, 3, 2, 4)
    input_grad = inputs.reshape(batch, channels, tokens).astype(jnp.bfloat16)
    total, last = sum_over_chan(total, chan)
    input_grad, last = lax.optimization_barrier((input_grad, last))
    total = total + last
    per_filter = channels // groups
    norm = float(tokens * devices * batch * per_filter * chan) ** -0.5
    filter_grad = total.swapaxes(1, 2).reshape(groups, tokens) * (norm / TOKENS)
    return input_grad, filter_grad


def solution(mesh):
    placed = (P(None, "chan", "ctx"), P(None, "chan", "ctx"), P(None, "ctx"))
    return jax.shard_map(
        local,
        mesh=mesh,
        in_specs=placed,
        out_specs=(P(None, "chan", "ctx"), P(None, "ctx")),
        check_vma=False,
    )
```
